32 devices in a mesh: grp: 8 (over z, x), own: 4 (over y, core).
Axes of the slice: x: 2, y: 2, z: 4, core: 2. Of those that a mesh axis runs over, the one named last changes fastest.
Arguments:
- queries: bfloat16 [2048, 768], P(('grp', 'own')), may hold values from -6 to 6
- projection: bfloat16 [768, 768], replicated, may hold values from -0.21875 to 0.21875
- lists: bfloat16 [1024, 256, 768], P(('grp', 'own')), may hold values from -6 to 6
- probes: int32 [2048, 8], P(('grp', 'own')), may hold values from 0 to 1023, as said below
- owner_map: int32 [1024], replicated, may hold values from 0 to 1023, as said below
Outputs:
- scores: float32 [2048, 8, 256], P(('grp', 'own'))
The draws below stay inside these ranges and needn't reach their ends.
Inputs may be any that keep to these rules, and one draw needn't show every extreme that they name: A permutation: list i is stored in slot owner_map[i], slots k * 32 to (k + 1) * 32 - 1 lying on the k-th device of grp+own. `probes`: a query's 8 list ids are distinct; the 64 queries of one device probe lists stored on any one device at most 32 times in all; all queries together probe any one stored list at most 32 times.
All inputs are finite; a program needn't handle non-finite values.
Results may differ from the reference program's by a relative error of at most 0.0003.
Values may be sent and summed in bfloat16 or wider, within the bound.
A program may use at most 64 MiB of HBM per device.

```python
import jax
import jax.numpy as jnp
from jax import lax

D = 768
LSIZE = 256
NPROBE = 8
LISTS_DEV = 32
Q_DEV = 64
NLIST = 1024
NQ = 2048


def probe_plan(key):
    device_count = NLIST // LISTS_DEV
    pair_count = Q_DEV * NPROBE
    mean_load = pair_count // device_count
    capacity = 2 * mean_load
    quarter = device_count // 4
    base = jax.random.fold_in(key, 7)
    key_map, key_rank, key_shift, key_order, key_rows, key_cols = jax.random.split(base, 6)
    slot_of = jax.random.permutation(key_map, NLIST).astype(jnp.int32)
    list_at = jnp.zeros((NLIST,), jnp.int32).at[slot_of].set(jnp.arange(NLIST, dtype=jnp.int32))
    ranked = jax.random.permutation(key_rank, device_count).astype(jnp.int32)
    shifts = jax.random.randint(key_shift, (device_count, quarter), 0, mean_load // 2 + 1).astype(jnp.int32)
    by_rank = jnp.concatenate([jnp.full((device_count, quarter), capacity, jnp.int32), 3 * mean_load // 2 - shifts, mean_load // 2 + shifts, jnp.zeros((device_count, device_count - 3 * quarter), jnp.int32)], axis=1)
    counts = jnp.zeros((device_count, device_count), jnp.int32).at[:, ranked].set(by_rank)
    orders = jax.vmap(lambda kk: jax.random.permutation(kk, device_count).astype(jnp.int32))(jax.random.split(key_order, device_count))
    row_keys = jax.random.split(key_rows, device_count)
    col_keys = jax.random.split(key_cols, device_count)

    def one_source(source, order_row, count_row, row_key, col_key):
        run_counts = count_row[order_row]
        target = jnp.repeat(order_row, run_counts, total_repeat_length=pair_count)
        starts = jnp.cumsum(run_counts) - run_counts
        run_index = jnp.repeat(jnp.arange(device_count, dtype=jnp.int32), run_counts, total_repeat_length=pair_count)
        within = jnp.arange(pair_count, dtype=jnp.int32) - starts[run_index]
        local = (source * capacity + within) % LISTS_DEV
        ids = list_at[target * LISTS_DEV + local]
        grid = ids.reshape(NPROBE, Q_DEV).T
        grid = grid[jax.random.permutation(row_key, Q_DEV)]
        grid = jax.vmap(lambda row, kk: row[jax.random.permutation(kk, NPROBE)])(grid, jax.random.split(col_key, Q_DEV))
        return grid
    grids = jax.vmap(one_source)(jnp.arange(device_count, dtype=jnp.int32), orders, counts, row_keys, col_keys)
    return (slot_of, grids.reshape(NQ, NPROBE).astype(jnp.int32))


def draw_probes(key, part):
    return probe_plan(key)[1]


def draw_owner_map(key, part):
    return probe_plan(key)[0]


def levels(stream_key, shape, shards, low, largest):
    gain = 1.0
    for dim, blocks in shards:
        heights = jax.random.uniform(jax.random.fold_in(jax.random.fold_in(stream_key, 6), dim), (blocks,), jnp.float32, low / len(shards), largest / len(shards))
        gain = gain * jnp.repeat(jnp.exp(heights), shape[dim] // blocks).reshape((-1,) + (1,) * (len(shape) - 1 - dim))
    return gain


def normal_values(rng, extent, width, reach, pieces=(), kind=jnp.bfloat16):
    values = width * jax.random.normal(rng, extent, jnp.float32)
    if pieces:
        values = values * levels(rng, extent, pieces, -0.22, 0.18)
    return jnp.clip(values, -reach, reach).astype(kind)


def setup_inputs(seed: int = 0) -> dict:
    splits = jax.random.split(jax.random.key(seed), 6)
    queries = normal_values(splits[0], (NQ, D), 1.0, 6.0, ((0, 32),))
    projection = normal_values(splits[1], (D, D), D ** -0.5, 0.21875)
    lists = normal_values(splits[2], (NLIST, LSIZE, D), 1.0, 6.0, ((0, 32),))
    probes = draw_probes(jax.random.fold_in(splits[5], 71), 0)
    owner_map = draw_owner_map(jax.random.fold_in(splits[5], 71), 0)
    return {"queries": queries, "projection": projection, "lists": lists, "probes": probes, "owner_map": owner_map}


def reference(queries, projection, lists, probes, owner_map):
    projected = jnp.dot(queries, projection, preferred_element_type=jnp.float32).astype(jnp.bfloat16)
    stored = jnp.take(owner_map, probes).astype(jnp.int32)
    block = 32
    query_blocks = projected.reshape(NQ // block, block, D)
    slot_blocks = stored.reshape(NQ // block, block, NPROBE)

    def one_block(args):
        rows, slots = args
        rows_f = rows.astype(jnp.float32)
        vectors = jnp.take(lists, slots.reshape(-1), axis=0).astype(jnp.float32)
        vectors = vectors.reshape(block, NPROBE, LSIZE, D)
        dots = jnp.einsum("qd,qjvd->qjv", rows_f, vectors)
        vec_norm = jnp.einsum("qjvd,qjvd->qjv", vectors, vectors)
        row_norm = jnp.sum(rows_f * rows_f, axis=1)
        return (row_norm[:, None, None] + vec_norm - 2.0 * dots) / D

    result = lax.map(one_block, (query_blocks, slot_blocks))
    return result.reshape(NQ, NPROBE, LSIZE)
```

```python
import jax
import jax.numpy as jnp
from jax import lax
from jax.experimental import pallas as pl
from jax.experimental.pallas import tpu as pltpu
from jax.sharding import PartitionSpec as P

AXES = ("grp", "own")
LANES = 128
LOG2E = 1.4426950408889634
LN2 = 0.6931471805599453


def select_kernel(queries, width, row_ref, all_ref, out_ref):
    devices = all_ref.shape[0]
    count = out_ref.shape[0]
    numbers = lax.broadcasted_iota(jnp.int32, (count, devices * queries), 1)
    pick = (numbers == row_ref[...]).astype(jnp.float32).astype(jnp.bfloat16)
    for j in range(width // LANES):
        part = all_ref[:, j * queries : (j + 1) * queries, :].reshape(devices * queries, LANES)
        out_ref[:, j * LANES : (j + 1) * LANES] = jnp.dot(
            pick, part, preferred_element_type=jnp.float32
        ).astype(jnp.bfloat16)


def select_rows(everyone, row_of, queries, width):
    slots = row_of.shape[0]
    block = min(256, slots)
    return pl.pallas_call(
        lambda *refs: select_kernel(queries, width, *refs),
        grid=(slots // block,),
        out_shape=jax.ShapeDtypeStruct((slots, width), jnp.bfloat16),
        in_specs=[
            pl.BlockSpec((block, 1), lambda i: (i, 0)),
            pl.BlockSpec(memory_space=pltpu.VMEM),
        ],
        out_specs=pl.BlockSpec((block, width), lambda i: (i, 0)),
        compiler_params=pltpu.CompilerParams(vmem_limit_bytes=48 * 2**20),
    )(row_of[:, None], everyone)


def score_kernel(blocks, rows_ref, lists_ref, spot_ref, out_ref, held):
    step = pl.program_id(0)
    count, list_size, width = lists_ref.shape
    capacity = rows_ref.shape[0] // count
    for n in range(count):
        rows = rows_ref[n * capacity : (n + 1) * capacity, :]
        dots = lax.dot_general(
            rows, lists_ref[n], (((1,), (1,)), ((), ())), preferred_element_type=jnp.float32
        )
        rows_f = rows.astype(jnp.float32)
        row_norm = jnp.sum(rows_f * rows_f, axis=1, keepdims=True)
        partial = None
        for j in range(width // LANES):
            part = lists_ref[n, :, j * LANES : (j + 1) * LANES].astype(jnp.float32)
            partial = part * part if partial is None else partial + part * part
        vec_norm = jnp.sum(partial.T, axis=0, keepdims=True)
        distance = jnp.maximum((row_norm + vec_norm - 2.0 * dots) / width, 0.0)
        largest = jnp.maximum(jnp.max(distance, axis=1, keepdims=True), 1e-30)
        power = jnp.clip(jnp.ceil(jnp.log(largest) * LOG2E + 1e-3), -100.0, 120.0)
        code = jnp.clip(jnp.round(distance * (65535.0 * jnp.exp(power * -LN2))), 0.0, 65535.0)
        high = jnp.floor(code * (1.0 / 256.0))
        low = code - high * 256.0
        place = pl.ds(pl.multiple_of((step * count + n) * capacity, 16), capacity)
        held[place, :list_size] = high.astype(jnp.bfloat16)
        held[place, list_size : 2 * list_size] = low.astype(jnp.bfloat16)
        held[place, 2 * list_size :] = jnp.broadcast_to(power, (capacity, LANES)).astype(
            jnp.bfloat16
        )

    @pl.when(step == pl.num_programs(0) - 1)
    def _():
        slots = held.shape[0]
        each = slots // blocks
        numbers = lax.broadcasted_iota(jnp.int32, (slots, slots), 1)
        pick = (numbers == spot_ref[...]).astype(jnp.float32).astype(jnp.bfloat16)
        got = jnp.dot(pick, held[...], preferred_element_type=jnp.float32)
        code = got[:, :list_size] * 256.0 + got[:, list_size : 2 * list_size] - 32768.0
        parts = [
            code[:, h * LANES : (h + 1) * LANES].reshape(blocks, each, LANES)
            for h in range(list_size // LANES)
        ]
        powers = got[:, 2 * list_size :].reshape(blocks, each, LANES)
        slot = lax.broadcasted_iota(jnp.int32, powers.shape, 1)
        lane = lax.broadcasted_iota(jnp.int32, powers.shape, 2)
        powers = jnp.sum(jnp.where(slot == lane, powers, 0.0), axis=1, keepdims=True)
        parts.append(jnp.broadcast_to(powers, (blocks, 16, LANES)))
        whole = jnp.concatenate(parts, axis=1)
        out_ref[...] = whole.astype(jnp.int32).astype(jnp.int16)


def score(grouped, lists, spot, blocks):
    list_count, list_size, width = lists.shape
    slots = grouped.shape[0]
    count = 4
    out_rows = (slots // blocks) * list_size // LANES + 16
    return pl.pallas_call(
        lambda *refs: score_kernel(blocks, *refs),
        grid=(list_count // count,),
        out_shape=jax.ShapeDtypeStruct((blocks, out_rows, LANES), jnp.int16),
        in_specs=[
            pl.BlockSpec((slots // list_count * count, width), lambda i: (i, 0)),
            pl.BlockSpec((count, list_size, width), lambda i: (i, 0, 0)),
            pl.BlockSpec((slots, 1), lambda i: (0, 0)),
        ],
        out_specs=pl.BlockSpec((blocks, out_rows, LANES), lambda i: (0, 0, 0)),
        scratch_shapes=[pltpu.VMEM((slots, 2 * list_size + LANES), jnp.bfloat16)],
        compiler_params=pltpu.CompilerParams(vmem_limit_bytes=40 * 2**20),
    )(grouped, lists, spot[:, None])


def exchange_kernel(device_count, owner_count, out_ref, in_ref, send_sem, recv_sem):
    me = lax.axis_index("grp") * owner_count + lax.axis_index("own")

    def at(k):
        other = lax.rem(me + k, device_count)
        return other, (other // owner_count, lax.rem(other, owner_count))

    barrier = pltpu.get_barrier_semaphore()

    @pl.loop(1, device_count)
    def _(k):
        pl.semaphore_signal(
            barrier, inc=1, device_id=at(k)[1], device_id_type=pl.DeviceIdType.MESH
        )

    pl.semaphore_wait(barrier, device_count - 1)

    def describe(k, block):
        other, where = at(k)
        return pltpu.make_async_remote_copy(
            src_ref=out_ref.at[other],
            dst_ref=in_ref.at[block],
            send_sem=send_sem.at[k],
            recv_sem=recv_sem.at[block],
            device_id=where,
            device_id_type=pl.DeviceIdType.MESH,
        )

    @pl.loop(1, device_count)
    def _(k):
        describe(k, me).start()

    in_ref[me] = out_ref[me]

    @pl.loop(1, device_count)
    def _(k):
        describe(k, at(k)[0]).wait_recv()

    @pl.loop(1, device_count)
    def _(k):
        describe(k, me).wait_send()


def exchange(blocks):
    owner_count = lax.axis_size("own")
    device_count = blocks.shape[0]
    return pl.pallas_call(
        lambda *refs: exchange_kernel(device_count, owner_count, *refs),
        out_shape=jax.ShapeDtypeStruct(blocks.shape, blocks.dtype),
        in_specs=[pl.BlockSpec(memory_space=pltpu.VMEM)],
        out_specs=pl.BlockSpec(memory_space=pltpu.VMEM),
        scratch_shapes=[
            pltpu.SemaphoreType.DMA((device_count,)),
            pltpu.SemaphoreType.DMA((device_count,)),
        ],
        compiler_params=pltpu.CompilerParams(
            collective_id=1, has_side_effects=True, vmem_limit_bytes=16 * 2**20
        ),
    )(blocks)


def general(queries, projection, lists, probes, owner_map):
    query_count, width = queries.shape
    probe_count = probes.shape[1]
    lists_here, list_size = lists.shape[0], lists.shape[1]
    device_count = lax.axis_size("grp") * lax.axis_size("own")
    pairs = query_count * probe_count
    capacity = 2 * pairs // device_count
    list_capacity = device_count * capacity // lists_here
    slots = device_count * capacity
    me = lax.axis_index(AXES)

    projected = jnp.dot(queries, projection, preferred_element_type=jnp.float32).astype(
        jnp.bfloat16
    )
    stored = jnp.take(owner_map, probes.reshape(-1))
    target = stored // lists_here
    local = stored % lists_here
    to_target = (target[:, None] == jnp.arange(device_count, dtype=jnp.int32)[None, :]).astype(
        jnp.bfloat16
    )
    step = jnp.arange(pairs, dtype=jnp.int32)
    earlier = (step[None, :] < step[:, None]).astype(jnp.bfloat16)
    before = jnp.dot(earlier, to_target, preferred_element_type=jnp.float32)
    rank = jnp.sum(before * to_target.astype(jnp.float32), axis=1).astype(jnp.int32)
    position = target * capacity + rank

    at_rank = (rank[:, None] == jnp.arange(capacity, dtype=jnp.int32)[None, :]).astype(jnp.bfloat16)
    query_of = step // probe_count
    what = jnp.stack([jnp.ones_like(step), query_of, local], axis=0).astype(jnp.bfloat16)
    weighted = to_target.T[None] * what[:, None, :]
    table = jnp.dot(
        weighted.reshape(3 * device_count, pairs), at_rank, preferred_element_type=jnp.float32
    ).reshape(3, device_count, capacity)
    table = jnp.where(table[:1] > 0.5, table[1:], -1.0).astype(jnp.bfloat16)
    columns = width // LANES
    extra = -(-(2 * slots) // (16 * LANES)) * 16
    table = jnp.pad(table.reshape(-1), (0, extra * LANES - 2 * slots)).reshape(extra, LANES)
    stacked = projected.reshape(query_count, columns, LANES).transpose(1, 0, 2)
    stacked = stacked.reshape(columns * query_count, LANES)

    everyone = lax.all_gather(jnp.concatenate([stacked, table], axis=0), AXES, tiled=False)
    tables = everyone[:, columns * query_count :].reshape(device_count, -1)[:, : 2 * slots]
    tables = tables.reshape(device_count, 2, device_count, capacity)
    mine = lax.dynamic_index_in_dim(tables, me, axis=2, keepdims=False).astype(jnp.int32)
    asked_query = mine[:, 0].reshape(-1)
    asked_list = mine[:, 1].reshape(-1)
    row_of = (
        asked_query + query_count * (jnp.arange(slots, dtype=jnp.int32) // capacity)
    )

    in_list = (asked_list[:, None] == jnp.arange(lists_here, dtype=jnp.int32)[None, :]).astype(
        jnp.bfloat16
    )
    place = jnp.arange(slots, dtype=jnp.int32)
    earlier = (place[None, :] < place[:, None]).astype(jnp.bfloat16)
    before = jnp.dot(earlier, in_list, preferred_element_type=jnp.float32)
    order = jnp.sum(before * in_list.astype(jnp.float32), axis=1).astype(jnp.int32)
    valid = asked_list >= 0
    spot = jnp.where(valid, asked_list * list_capacity + order, -1)
    hit = spot[:, None] == jnp.arange(lists_here * list_capacity, dtype=jnp.int32)[None, :]
    grouped_row = jnp.sum(jnp.where(hit, row_of[:, None], 0), axis=0)
    grouped = select_rows(everyone, grouped_row, query_count, width)
    blocks = score(grouped, lists, spot, device_count)
    answer_rows = capacity * list_size // LANES
    got = exchange(blocks).astype(jnp.float32)
    powers = got[:, answer_rows:].reshape(device_count, -1)[:, :capacity].reshape(slots, 1)
    returned = (
        got[:, :answer_rows]
        .reshape(device_count, list_size // LANES, capacity, LANES)
        .transpose(0, 2, 1, 3)
        .reshape(slots, list_size)
    )
    returned = (returned + 32768.0) * (jnp.exp2(powers) / 65535.0)
    return returned[position].reshape(query_count, probe_count, list_size)


PLANES = 4
PLANE = 8
TABLE = 16
CHUNK = 8


def number(z, x, y, c):
    return z * PLANE + x * 4 + y * 2 + c


def mesh_id(n):
    return (n // 4, lax.rem(n, 4))


def ranks(mine):
    rows = mine.shape[0]
    lane_a = lax.broadcasted_iota(jnp.int32, (LANES, LANES), 0)
    lane_b = lax.broadcasted_iota(jnp.int32, (LANES, LANES), 1)
    upper = jnp.where(lane_a < lane_b, 1.0, 0.0).astype(jnp.bfloat16)
    ones = jnp.ones((LANES, LANES), jnp.bfloat16)
    row_a = lax.broadcasted_iota(jnp.int32, (rows, rows), 0)
    row_b = lax.broadcasted_iota(jnp.int32, (rows, rows), 1)
    lower = jnp.where((row_a // 8 == row_b // 8) & (row_b < row_a), 1.0, 0.0).astype(jnp.bfloat16)
    narrow = mine.astype(jnp.bfloat16)
    within = jnp.dot(narrow, upper, preferred_element_type=jnp.float32)
    totals = jnp.dot(narrow, ones, preferred_element_type=jnp.float32).astype(jnp.bfloat16)
    return within + jnp.dot(lower, totals, preferred_element_type=jnp.float32)


def fused_kernel(
    queries_ref,
    projection_ref,
    probes_ref,
    owner_ref,
    lists_hbm,
    out_ref,
    all_ref,
    lists_ref,
    norms_ref,
    picked_ref,
    send_ref,
    got_ref,
    place_ref,
    list_sem,
    spread_send,
    spread_recv,
    back_send,
    back_recv,
):
    grp, own = lax.axis_index("grp"), lax.axis_index("own")
    z, x, y, c = grp // 2, lax.rem(grp, 2), own // 2, lax.rem(own, 2)
    me = number(z, x, y, c)
    inside = x * 4 + y * 2 + c
    devices = all_ref.shape[0]
    query_count, width = queries_ref.shape
    list_count, list_size = lists_ref.shape[0], lists_ref.shape[1]
    columns = width // LANES
    table_at = columns * query_count
    capacity = 32

    barrier = pltpu.get_barrier_semaphore()

    @pl.loop(1, devices)
    def _(k):
        pl.semaphore_signal(
            barrier,
            inc=1,
            device_id=mesh_id(lax.rem(me + k, devices)),
            device_id_type=pl.DeviceIdType.MESH,
        )

    part = list_count // list_sem.shape[0]

    def list_copy(n):
        piece = pl.ds(n * part, part)
        return pltpu.make_async_copy(lists_hbm.at[piece], lists_ref.at[piece], list_sem.at[n])

    for n in range(list_sem.shape[0]):
        list_copy(n).start()

    projected = jnp.dot(
        queries_ref[...], projection_ref[...], preferred_element_type=jnp.float32
    ).astype(jnp.bfloat16)
    for j in range(columns):
        all_ref[me, j * query_count : (j + 1) * query_count, :] = projected[
            :, j * LANES : (j + 1) * LANES
        ]
    ids = jnp.concatenate([probes_ref[...], probes_ref[...]], axis=1)
    low, high = ids & (LANES - 1), ids >> 7
    stored = jnp.zeros_like(ids)
    for h in range(owner_ref.shape[0]):
        row = jnp.broadcast_to(owner_ref[h : h + 1, :], ids.shape)
        found = jnp.take_along_axis(row, low, axis=1, mode="promise_in_bounds")
        stored = jnp.where(high == h, found, stored)
    lane8 = lax.broadcasted_iota(jnp.int32, ids.shape, 1)
    table = jnp.where(lane8 < query_count, stored >> 5, stored & 31).astype(jnp.float32)
    all_ref[me, table_at:, :] = jnp.concatenate([table, jnp.zeros_like(table)], axis=0).astype(
        jnp.bfloat16
    )
    pl.semaphore_wait(barrier, devices - 1)

    first = 3 * (1 - z // 2)
    last = 1 + lax.rem(z, 2)
    planes = [z, first, 6 - z - first - last, last]
    xa, ya = x * c + (1 - x) * (1 - c), y * (1 - c) + (1 - y) * c
    xb, yb = x * (1 - c) + (1 - x) * c, y * c + (1 - y) * (1 - c)
    peer_a, peer_b = number(z, xa, ya, c), number(z, xb, yb, c)
    sibling = number(z, x, y, 1 - c)
    sent = []

    def describe(block, peer, slot):
        return pltpu.make_async_remote_copy(
            src_ref=all_ref.at[block],
            dst_ref=all_ref.at[block],
            send_sem=spread_send.at[slot],
            recv_sem=spread_recv.at[block],
            device_id=mesh_id(peer),
            device_id_type=pl.DeviceIdType.MESH,
        )

    def send(block, peer):
        copy = describe(block, peer, len(sent))
        copy.start()
        sent.append(copy)

    def arrived(block):
        describe(block, sibling, 0).wait_recv()

    def relay_column(p):
        block = number(p, x, y, c)
        arrived(block)
        send(block, peer_a)
        send(block, peer_b)
        send(block, sibling)

    def relay_a(p):
        block = number(p, xa, ya, c)
        arrived(block)
        send(block, peer_b)
        send(block, sibling)

    def relay_b(p):
        block = number(p, xb, yb, c)
        arrived(block)
        send(block, sibling)

    def relay_diagonal(p):
        block = number(p, 1 - x, 1 - y, c)
        arrived(block)
        send(block, sibling)

    def complete(p):
        for xx, yy in ((x, y), (xa, ya), (xb, yb), (1 - x, 1 - y)):
            arrived(number(p, xx, yy, 1 - c))

    send(me, peer_a)
    send(me, peer_b)
    for p in planes[1:]:
        send(me, number(p, x, y, c))
    send(me, sibling)

    def list_norms(n):
        list_copy(n).wait()
        rows = []
        for i in range(n * part, (n + 1) * part):
            partial = None
            for j in range(columns):
                piece = lists_ref[i, :, j * LANES : (j + 1) * LANES].astype(jnp.float32)
                partial = piece * piece if partial is None else partial + piece * piece
            rows.append(0.5 * jnp.sum(partial.T, axis=0, keepdims=True))
        norms_ref[n * part : (n + 1) * part, :] = jnp.concatenate(rows, axis=0)

    steps = {
        3: lambda: relay_a(planes[0]),
        4: lambda: relay_b(planes[0]),
        5: lambda: relay_column(planes[1]),
        6: lambda: relay_diagonal(planes[0]),
    }
    for n in range(list_sem.shape[0]):
        list_norms(n)
        if n in steps:
            steps[n]()

    def back(target, block):
        return pltpu.make_async_remote_copy(
            src_ref=send_ref.at[target],
            dst_ref=got_ref.at[block],
            send_sem=back_send.at[target],
            recv_sem=back_recv.at[block],
            device_id=mesh_id(target),
            device_id_type=pl.DeviceIdType.MESH,
        )

    me_f = me.astype(jnp.float32)
    slots = PLANE * capacity
    ones = jnp.ones((LANES, LANES), jnp.bfloat16)
    slot = lax.broadcasted_iota(jnp.int32, (capacity, LANES), 0).astype(jnp.float32)

    def choose(p):
        tables = all_ref[pl.ds(p * PLANE, PLANE), table_at:, :].astype(jnp.float32)
        tables = tables[:, :8, :].reshape(PLANE * 8, LANES)
        lane = lax.broadcasted_iota(jnp.int32, tables.shape, 1)
        mine = jnp.where((lane < query_count) & (tables == me_f), 1.0, 0.0)
        rank = jnp.where(mine > 0.5, ranks(mine), -1.0)
        local = tables + 1.0
        at = (rank, pltpu.roll(rank, query_count, 1))
        what = (pltpu.roll(local, query_count, 1), local)
        picks, lists_of = [], []
        for t in range(PLANE):
            pick = jnp.zeros((capacity, LANES), jnp.float32)
            which = jnp.zeros((capacity, LANES), jnp.float32)
            for j in range(8):
                row = t * 8 + j
                hit = at[t % 2][row : row + 1, :] == slot
                pick = jnp.where(hit, 1.0, pick)
                which = jnp.where(hit, what[t % 2][row : row + 1, :], which)
            picks.append(pick.astype(jnp.bfloat16))
            lists_of.append(which.astype(jnp.bfloat16))
        place = jnp.dot(
            jnp.concatenate(lists_of, axis=0), ones, preferred_element_type=jnp.float32
        )
        norm = jnp.zeros((slots, LANES), jnp.float32)
        for j in range(columns):
            rows = []
            for u in range(PLANE // 2):
                pair = all_ref[
                    pl.ds(p * PLANE + 2 * u, 2), j * query_count : (j + 1) * query_count, :
                ].reshape(2 * query_count, LANES)
                pick = jnp.concatenate(picks[2 * u : 2 * u + 2], axis=0)
                rows.append(jnp.dot(pick, pair, preferred_element_type=jnp.float32))
            piece = jnp.concatenate(rows, axis=0)
            norm = norm + piece * piece
            picked_ref[:, j * LANES : (j + 1) * LANES] = piece.astype(jnp.bfloat16)
        return place, jnp.sum(norm, axis=1, keepdims=True)

    def encode(p, best, norm):
        distance = jnp.maximum((norm - 2.0 * best) * (1.0 / width), 0.0)
        largest = jnp.maximum(jnp.max(distance, axis=1, keepdims=True), 1e-30)
        power = jnp.clip(jnp.ceil(jnp.log(largest) * LOG2E + 1e-3), -100.0, 120.0)
        code = jnp.clip(jnp.round(distance * (65535.0 * jnp.exp(power * -LN2))), 0.0, 65535.0)
        code = code.astype(jnp.int32)
        word = code[:, :LANES] | (code[:, LANES:] << 16)
        here = pl.ds(p * PLANE, PLANE)
        send_ref[here, :capacity, :] = word.reshape(PLANE, capacity, LANES)
        spot = lax.broadcasted_iota(jnp.int32, (PLANE, capacity, LANES), 1) + own * capacity
        lane = lax.broadcasted_iota(jnp.int32, (PLANE, capacity, LANES), 2)
        powers = jnp.broadcast_to(power, (slots, LANES)).reshape(PLANE, capacity, LANES)
        powers = jnp.sum(jnp.where(spot == lane, powers, 0.0), axis=1, keepdims=True)
        send_ref[here, capacity : capacity + 1, :] = powers.astype(jnp.int32)

    relay_after = {}
    for k in range(PLANES - 1):
        later = planes[k + 1]
        relay_after[k, 0] = [lambda p=later: relay_a(p)]
        relay_after[k, 1] = [lambda p=later: relay_b(p)]
        if k + 2 < PLANES:
            relay_after[k, 1].append(lambda p=planes[k + 2]: relay_column(p))
        relay_after[k, 2] = [lambda p=later: relay_diagonal(p)]

    returned = []
    for k, p in enumerate(planes):
        complete(p)
        place, norm = choose(p)
        best = jnp.zeros((slots, list_size), jnp.float32)
        for g in range(list_count // CHUNK):
            dots = lax.dot_general(
                picked_ref[...],
                lists_ref[g * CHUNK : (g + 1) * CHUNK].reshape(CHUNK * list_size, width),
                (((1,), (1,)), ((), ())),
                preferred_element_type=jnp.float32,
            )
            for i in range(CHUNK):
                n = g * CHUNK + i
                hit = place == n + 1.0
                hit = jnp.concatenate([hit] * (list_size // LANES), axis=1)
                value = dots[:, i * list_size : (i + 1) * list_size] - norms_ref[n : n + 1, :]
                best = jnp.where(hit, value, best)
            for step in relay_after.get((k, g), []):
                step()
        encode(p, best, norm)
        for i in range(1 if k == 0 else 0, PLANE):
            target = p * PLANE + lax.rem(inside + i, PLANE)
            copy = back(target, me)
            copy.start()
            returned.append(copy)
    got_ref[me] = send_ref[me]

    target = jnp.where(lane8 < query_count, (stored >> 5).astype(jnp.float32), -1.0)
    mine = jnp.concatenate(
        [jnp.where(target == float(d), 1.0, 0.0) for d in range(devices)], axis=0
    )
    rank = ranks(mine)
    spot = jnp.zeros(ids.shape, jnp.float32)
    for d in range(devices):
        spot = jnp.where(target == float(d), rank[d * 8 : (d + 1) * 8] + float(d * capacity), spot)
    wide = lax.broadcasted_iota(jnp.int32, (8, devices * capacity), 1).astype(jnp.float32)
    for q in range(0, query_count, 2):
        both = [jnp.where(spot[:, i : i + 1] == wide, 1.0, 0.0) for i in (q, q + 1)]
        place_ref[q * 8 : (q + 2) * 8, :] = jnp.concatenate(both, axis=0).astype(jnp.bfloat16)

    for p in planes:
        for i in range(PLANE):
            block = p * PLANE + lax.rem(inside + i, PLANE)
            if p is not planes[0] or i > 0:
                back(block, block).wait_recv()

    words = got_ref[:, :capacity, :].reshape(devices * capacity, LANES)
    pieces = [(words >> s) & 255 for s in (0, 8, 16, 24)]
    pieces = [piece.astype(jnp.float32).astype(jnp.bfloat16) for piece in pieces]
    powers = got_ref[:, capacity : capacity + 1, :].astype(jnp.float32)
    powers = jnp.sum(powers.reshape(devices // 4, 4, LANES), axis=1)
    powers = jnp.concatenate(
        [jnp.broadcast_to(powers[g : g + 1, :], (LANES, LANES)) for g in range(devices // 4)],
        axis=1,
    ).astype(jnp.bfloat16)
    chosen = jnp.dot(
        place_ref[...], jnp.concatenate(pieces, axis=1), preferred_element_type=jnp.float32
    )
    power = lax.dot_general(
        place_ref[...], powers, (((1,), (1,)), ((), ())), preferred_element_type=jnp.float32
    )
    scale = jnp.exp(power * LN2) * (1.0 / 65535.0)
    for h in range(2):
        low = chosen[:, 2 * h * LANES : (2 * h + 1) * LANES]
        high = chosen[:, (2 * h + 1) * LANES : (2 * h + 2) * LANES]
        out_ref[:, h * LANES : (h + 1) * LANES] = (low + 256.0 * high) * scale

    for copy in sent:
        copy.wait_send()
    for copy in returned:
        copy.wait_send()


def fused(queries, projection, lists, probes, owner_map):
    query_count, width = queries.shape
    probe_count = probes.shape[1]
    list_count, list_size = lists.shape[0], lists.shape[1]
    devices, capacity = PLANES * PLANE, 32
    rows = width // LANES * query_count + TABLE
    vmem = pl.BlockSpec(memory_space=pltpu.VMEM)
    scores = pl.pallas_call(
        fused_kernel,
        out_shape=jax.ShapeDtypeStruct((query_count * probe_count, list_size), jnp.float32),
        in_specs=[vmem, vmem, vmem, vmem, pl.BlockSpec(memory_space=pl.ANY)],
        out_specs=vmem,
        scratch_shapes=[
            pltpu.VMEM((devices, rows, LANES), jnp.bfloat16),
            pltpu.VMEM(lists.shape, jnp.bfloat16),
            pltpu.VMEM((list_count, list_size), jnp.float32),
            pltpu.VMEM((PLANE * capacity, width), jnp.bfloat16),
            pltpu.VMEM((devices, capacity + 1, LANES), jnp.int32),
            pltpu.VMEM((devices, capacity + 1, LANES), jnp.int32),
            pltpu.VMEM((query_count * probe_count, devices * capacity), jnp.bfloat16),
            pltpu.SemaphoreType.DMA((8,)),
            pltpu.SemaphoreType.DMA((devices,)),
            pltpu.SemaphoreType.DMA((devices,)),
            pltpu.SemaphoreType.DMA((devices,)),
            pltpu.SemaphoreType.DMA((devices,)),
        ],
        compiler_params=pltpu.CompilerParams(
            collective_id=0, has_side_effects=True, vmem_limit_bytes=52 * 2**20
        ),
    )(queries, projection, probes.T, owner_map.reshape(-1, LANES), lists)
    return scores.reshape(query_count, probe_count, list_size)


def solution(mesh):
    placed = (
        P(AXES, None),
        P(),
        P(AXES, None, None),
        P(AXES, None),
        P(),
    )
    sizes = (mesh.shape["grp"], mesh.shape["own"])
    return jax.shard_map(
        fused if sizes == (8, 4) else general,
        mesh=mesh,
        in_specs=placed,
        out_specs=P(AXES, None, None),
        check_vma=False,
    )
```

```python
import jax
import jax.numpy as jnp
from jax import lax
from jax.experimental import pallas as pl
from jax.experimental.pallas import tpu as pltpu
from jax.sharding import PartitionSpec as P

AXES = ("grp", "own")
LANES = 128
LOG2E = 1.4426950408889634
LN2 = 0.6931471805599453


def select_kernel(queries, width, row_ref, all_ref, out_ref):
    devices = all_ref.shape[0]
    count = out_ref.shape[0]
    numbers = lax.broadcasted_iota(jnp.int32, (count, devices * queries), 1)
    pick = (numbers == row_ref[...]).astype(jnp.float32).astype(jnp.bfloat16)
    for j in range(width // LANES):
        part = all_ref[:, j * queries : (j + 1) * queries, :].reshape(devices * queries, LANES)
        out_ref[:, j * LANES : (j + 1) * LANES] = jnp.dot(
            pick, part, preferred_element_type=jnp.float32
        ).astype(jnp.bfloat16)


def select_rows(everyone, row_of, queries, width):
    slots = row_of.shape[0]
    block = min(256, slots)
    return pl.pallas_call(
        lambda *refs: select_kernel(queries, width, *refs),
        grid=(slots // block,),
        out_shape=jax.ShapeDtypeStruct((slots, width), jnp.bfloat16),
        in_specs=[
            pl.BlockSpec((block, 1), lambda i: (i, 0)),
            pl.BlockSpec(memory_space=pltpu.VMEM),
        ],
        out_specs=pl.BlockSpec((block, width), lambda i: (i, 0)),
        compiler_params=pltpu.CompilerParams(vmem_limit_bytes=48 * 2**20),
    )(row_of[:, None], everyone)


def score_kernel(blocks, rows_ref, lists_ref, spot_ref, out_ref, held):
    step = pl.program_id(0)
    count, list_size, width = lists_ref.shape
    capacity = rows_ref.shape[0] // count
    for n in range(count):
        rows = rows_ref[n * capacity : (n + 1) * capacity, :]
        dots = lax.dot_general(
            rows, lists_ref[n], (((1,), (1,)), ((), ())), preferred_element_type=jnp.float32
        )
        rows_f = rows.astype(jnp.float32)
        row_norm = jnp.sum(rows_f * rows_f, axis=1, keepdims=True)
        partial = None
        for j in range(width // LANES):
            part = lists_ref[n, :, j * LANES : (j + 1) * LANES].astype(jnp.float32)
            partial = part * part if partial is None else partial + part * part
        vec_norm = jnp.sum(partial.T, axis=0, keepdims=True)
        distance = jnp.maximum((row_norm + vec_norm - 2.0 * dots) / width, 0.0)
        largest = jnp.maximum(jnp.max(distance, axis=1, keepdims=True), 1e-30)
        power = jnp.clip(jnp.ceil(jnp.log(largest) * LOG2E + 1e-3), -100.0, 120.0)
        code = jnp.clip(jnp.round(distance * (65535.0 * jnp.exp(power * -LN2))), 0.0, 65535.0)
        high = jnp.floor(code * (1.0 / 256.0))
        low = code - high * 256.0
        place = pl.ds(pl.multiple_of((step * count + n) * capacity, 16), capacity)
        held[place, :list_size] = high.astype(jnp.bfloat16)
        held[place, list_size : 2 * list_size] = low.astype(jnp.bfloat16)
        held[place, 2 * list_size :] = jnp.broadcast_to(power, (capacity, LANES)).astype(
            jnp.bfloat16
        )

    @pl.when(step == pl.num_programs(0) - 1)
    def _():
        slots = held.shape[0]
        each = slots // blocks
        numbers = lax.broadcasted_iota(jnp.int32, (slots, slots), 1)
        pick = (numbers == spot_ref[...]).astype(jnp.float32).astype(jnp.bfloat16)
        got = jnp.dot(pick, held[...], preferred_element_type=jnp.float32)
        code = got[:, :list_size] * 256.0 + got[:, list_size : 2 * list_size] - 32768.0
        parts = [
            code[:, h * LANES : (h + 1) * LANES].reshape(blocks, each, LANES)
            for h in range(list_size // LANES)
        ]
        powers = got[:, 2 * list_size :].reshape(blocks, each, LANES)
        slot = lax.broadcasted_iota(jnp.int32, powers.shape, 1)
        lane = lax.broadcasted_iota(jnp.int32, powers.shape, 2)
        powers = jnp.sum(jnp.where(slot == lane, powers, 0.0), axis=1, keepdims=True)
        parts.append(jnp.broadcast_to(powers, (blocks, 16, LANES)))
        whole = jnp.concatenate(parts, axis=1)
        out_ref[...] = whole.astype(jnp.int32).astype(jnp.int16)


def score(grouped, lists, spot, blocks):
    list_count, list_size, width = lists.shape
    slots = grouped.shape[0]
    count = 4
    out_rows = (slots // blocks) * list_size // LANES + 16
    return pl.pallas_call(
        lambda *refs: score_kernel(blocks, *refs),
        grid=(list_count // count,),
        out_shape=jax.ShapeDtypeStruct((blocks, out_rows, LANES), jnp.int16),
        in_specs=[
            pl.BlockSpec((slots // list_count * count, width), lambda i: (i, 0)),
            pl.BlockSpec((count, list_size, width), lambda i: (i, 0, 0)),
            pl.BlockSpec((slots, 1), lambda i: (0, 0)),
        ],
        out_specs=pl.BlockSpec((blocks, out_rows, LANES), lambda i: (0, 0, 0)),
        scratch_shapes=[pltpu.VMEM((slots, 2 * list_size + LANES), jnp.bfloat16)],
        compiler_params=pltpu.CompilerParams(vmem_limit_bytes=40 * 2**20),
    )(grouped, lists, spot[:, None])


def exchange_kernel(device_count, owner_count, out_ref, in_ref, send_sem, recv_sem):
    me = lax.axis_index("grp") * owner_count + lax.axis_index("own")

    def at(k):
        other = lax.rem(me + k, device_count)
        return other, (other // owner_count, lax.rem(other, owner_count))

    barrier = pltpu.get_barrier_semaphore()

    @pl.loop(1, device_count)
    def _(k):
        pl.semaphore_signal(
            barrier, inc=1, device_id=at(k)[1], device_id_type=pl.DeviceIdType.MESH
        )

    pl.semaphore_wait(barrier, device_count - 1)

    def describe(k, block):
        other, where = at(k)
        return pltpu.make_async_remote_copy(
            src_ref=out_ref.at[other],
            dst_ref=in_ref.at[block],
            send_sem=send_sem.at[k],
            recv_sem=recv_sem.at[block],
            device_id=where,
            device_id_type=pl.DeviceIdType.MESH,
        )

    @pl.loop(1, device_count)
    def _(k):
        describe(k, me).start()

    in_ref[me] = out_ref[me]

    @pl.loop(1, device_count)
    def _(k):
        describe(k, at(k)[0]).wait_recv()

    @pl.loop(1, device_count)
    def _(k):
        describe(k, me).wait_send()


def exchange(blocks):
    owner_count = lax.axis_size("own")
    device_count = blocks.shape[0]
    return pl.pallas_call(
        lambda *refs: exchange_kernel(device_count, owner_count, *refs),
        out_shape=jax.ShapeDtypeStruct(blocks.shape, blocks.dtype),
        in_specs=[pl.BlockSpec(memory_space=pltpu.VMEM)],
        out_specs=pl.BlockSpec(memory_space=pltpu.VMEM),
        scratch_shapes=[
            pltpu.SemaphoreType.DMA((device_count,)),
            pltpu.SemaphoreType.DMA((device_count,)),
        ],
        compiler_params=pltpu.CompilerParams(
            collective_id=1, has_side_effects=True, vmem_limit_bytes=16 * 2**20
        ),
    )(blocks)


def general(queries, projection, lists, probes, owner_map):
    query_count, width = queries.shape
    probe_count = probes.shape[1]
    lists_here, list_size = lists.shape[0], lists.shape[1]
    device_count = lax.axis_size("grp") * lax.axis_size("own")
    pairs = query_count * probe_count
    capacity = 2 * pairs // device_count
    list_capacity = device_count * capacity // lists_here
    slots = device_count * capacity
    me = lax.axis_index(AXES)

    projected = jnp.dot(queries, projection, preferred_element_type=jnp.float32).astype(
        jnp.bfloat16
    )
    stored = jnp.take(owner_map, probes.reshape(-1))
    target = stored // lists_here
    local = stored % lists_here
    to_target = (target[:, None] == jnp.arange(device_count, dtype=jnp.int32)[None, :]).astype(
        jnp.bfloat16
    )
    step = jnp.arange(pairs, dtype=jnp.int32)
    earlier = (step[None, :] < step[:, None]).astype(jnp.bfloat16)
    before = jnp.dot(earlier, to_target, preferred_element_type=jnp.float32)
    rank = jnp.sum(before * to_target.astype(jnp.float32), axis=1).astype(jnp.int32)
    position = target * capacity + rank

    at_rank = (rank[:, None] == jnp.arange(capacity, dtype=jnp.int32)[None, :]).astype(jnp.bfloat16)
    query_of = step // probe_count
    what = jnp.stack([jnp.ones_like(step), query_of, local], axis=0).astype(jnp.bfloat16)
    weighted = to_target.T[None] * what[:, None, :]
    table = jnp.dot(
        weighted.reshape(3 * device_count, pairs), at_rank, preferred_element_type=jnp.float32
    ).reshape(3, device_count, capacity)
    table = jnp.where(table[:1] > 0.5, table[1:], -1.0).astype(jnp.bfloat16)
    columns = width // LANES
    extra = -(-(2 * slots) // (16 * LANES)) * 16
    table = jnp.pad(table.reshape(-1), (0, extra * LANES - 2 * slots)).reshape(extra, LANES)
    stacked = projected.reshape(query_count, columns, LANES).transpose(1, 0, 2)
    stacked = stacked.reshape(columns * query_count, LANES)

    everyone = lax.all_gather(jnp.concatenate([stacked, table], axis=0), AXES, tiled=False)
    tables = everyone[:, columns * query_count :].reshape(device_count, -1)[:, : 2 * slots]
    tables = tables.reshape(device_count, 2, device_count, capacity)
    mine = lax.dynamic_index_in_dim(tables, me, axis=2, keepdims=False).astype(jnp.int32)
    asked_query = mine[:, 0].reshape(-1)
    asked_list = mine[:, 1].reshape(-1)
    row_of = (
        asked_query + query_count * (jnp.arange(slots, dtype=jnp.int32) // capacity)
    )

    in_list = (asked_list[:, None] == jnp.arange(lists_here, dtype=jnp.int32)[None, :]).astype(
        jnp.bfloat16
    )
    place = jnp.arange(slots, dtype=jnp.int32)
    earlier = (place[None, :] < place[:, None]).astype(jnp.bfloat16)
    before = jnp.dot(earlier, in_list, preferred_element_type=jnp.float32)
    order = jnp.sum(before * in_list.astype(jnp.float32), axis=1).astype(jnp.int32)
    valid = asked_list >= 0
    spot = jnp.where(valid, asked_list * list_capacity + order, -1)
    hit = spot[:, None] == jnp.arange(lists_here * list_capacity, dtype=jnp.int32)[None, :]
    grouped_row = jnp.sum(jnp.where(hit, row_of[:, None], 0), axis=0)
    grouped = select_rows(everyone, grouped_row, query_count, width)
    blocks = score(grouped, lists, spot, device_count)
    answer_rows = capacity * list_size // LANES
    got = exchange(blocks).astype(jnp.float32)
    powers = got[:, answer_rows:].reshape(device_count, -1)[:, :capacity].reshape(slots, 1)
    returned = (
        got[:, :answer_rows]
        .reshape(device_count, list_size // LANES, capacity, LANES)
        .transpose(0, 2, 1, 3)
        .reshape(slots, list_size)
    )
    returned = (returned + 32768.0) * (jnp.exp2(powers) / 65535.0)
    return returned[position].reshape(query_count, probe_count, list_size)


PLANES = 4
PLANE = 8
TABLE = 16
CHIPS = 4
CAPACITY = 32
VMEM_LIMIT = 56 * 2**20


def number(z, x, y, c):
    return z * PLANE + x * 4 + y * 2 + c


def mesh_id(n):
    return (n // 4, lax.rem(n, 4))


def ranks(mine):
    lane = lax.broadcasted_iota(jnp.int32, mine.shape, 1)
    within = mine
    for reach in (1, 2, 4, 8, 16, 32, 64):
        within = within + jnp.where(lane >= reach, pltpu.roll(within, reach, 1), 0.0)
    totals = jnp.broadcast_to(within[:, LANES - 1 :], mine.shape).reshape(-1, 8, LANES)
    probe = lax.broadcasted_iota(jnp.int32, totals.shape, 1)
    before = totals
    for reach in (1, 2, 4):
        before = before + jnp.where(probe >= reach, pltpu.roll(before, reach, 1), 0.0)
    return within - mine + (before - totals).reshape(mine.shape)


def fused_kernel(
    queries_hbm,
    projection_hbm,
    probes_hbm,
    owner_hbm,
    lists_hbm,
    out_hbm,
    queries_ref,
    projection_ref,
    probes_ref,
    owner_ref,
    all_ref,
    lists_ref,
    norms_ref,
    even_ref,
    odd_ref,
    send_ref,
    got_ref,
    place_ref,
    total_ref,
    out_ref,
    input_sem,
    list_sem,
    spread_send,
    spread_recv,
    back_send,
    back_recv,
    out_sem,
):
    grp, own = lax.axis_index("grp"), lax.axis_index("own")
    z, x, y, c = grp // 2, lax.rem(grp, 2), own // 2, lax.rem(own, 2)
    me = number(z, x, y, c)
    devices = all_ref.shape[0]
    query_count, width = queries_ref.shape
    list_count, list_size = lists_ref.shape[0], lists_ref.shape[1]
    columns = width // LANES
    table_at = columns * query_count
    capacity = CAPACITY

    inputs = [
        pltpu.make_async_copy(src, dst, input_sem.at[i])
        for i, (src, dst) in enumerate(
            (
                (projection_hbm, projection_ref),
                (queries_hbm, queries_ref),
                (probes_hbm, probes_ref),
                (owner_hbm, owner_ref),
            )
        )
    ]
    for copy in inputs:
        copy.start()
    barrier = pltpu.get_barrier_semaphore()

    @pl.loop(1, devices)
    def _(k):
        pl.semaphore_signal(
            barrier,
            inc=1,
            device_id=mesh_id(lax.rem(me + k, devices)),
            device_id_type=pl.DeviceIdType.MESH,
        )

    part = list_count // list_sem.shape[0]

    def list_copy(n):
        piece = pl.ds(n * part, part)
        return pltpu.make_async_copy(lists_hbm.at[piece], lists_ref.at[piece], list_sem.at[n])

    for n in range(list_sem.shape[0]):
        list_copy(n).start()
    for copy in inputs:
        copy.wait()

    projected = jnp.dot(
        queries_ref[...], projection_ref[...], preferred_element_type=jnp.float32
    ).astype(jnp.bfloat16)
    for j in range(columns):
        all_ref[me, j * query_count : (j + 1) * query_count, :] = projected[
            :, j * LANES : (j + 1) * LANES
        ]
    ids = jnp.concatenate([probes_ref[...], probes_ref[...]], axis=1)
    low, high = ids & (LANES - 1), ids >> 7
    stored = jnp.zeros_like(ids)
    for h in range(owner_ref.shape[0]):
        row = jnp.broadcast_to(owner_ref[h : h + 1, :], ids.shape)
        found = jnp.take_along_axis(row, low, axis=1, mode="promise_in_bounds")
        stored = jnp.where(high == h, found, stored)
    lane8 = lax.broadcasted_iota(jnp.int32, ids.shape, 1)
    table = jnp.where(lane8 < query_count, stored >> 5, stored & 31).astype(jnp.float32)
    all_ref[me, table_at:, :] = jnp.concatenate([table, jnp.zeros_like(table)], axis=0).astype(
        jnp.bfloat16
    )
    pl.semaphore_wait(barrier, devices - 1)

    near, cross, opposite = z + 1 - 2 * lax.rem(z, 2), lax.rem(z + 2, PLANES), PLANES - 1 - z
    xa, ya = x * c + (1 - x) * (1 - c), y * (1 - c) + (1 - y) * c
    xb, yb = x * (1 - c) + (1 - x) * c, y * c + (1 - y) * (1 - c)
    sides = {"o": (x, y), "a": (xa, ya), "b": (xb, yb), "d": (1 - x, 1 - y)}
    sides |= {"x": (1 - x, y), "y": (x, 1 - y)}

    def block_of(p, side):
        return number(p, *sides[side], c)

    def twin_of(p, side):
        return number(p, *sides[side], 1 - c)

    peer_a, peer_b = block_of(z, "a"), block_of(z, "b")
    peer_near, peer_cross = block_of(near, "o"), block_of(cross, "o")
    sibling = twin_of(z, "o")
    sent = []

    def describe(block, peer, slot):
        return pltpu.make_async_remote_copy(
            src_ref=all_ref.at[block],
            dst_ref=all_ref.at[block],
            send_sem=spread_send.at[slot],
            recv_sem=spread_recv.at[block],
            device_id=mesh_id(peer),
            device_id_type=pl.DeviceIdType.MESH,
        )

    def send(block, *peers):
        for peer in peers:
            copy = describe(block, peer, len(sent))
            copy.start()
            sent.append(copy)

    def arrived(block):
        describe(block, sibling, 0).wait_recv()

    def relay(p, side, *peers):
        arrived(block_of(p, side))
        send(block_of(p, side), *peers)

    send(me, peer_cross, peer_a, peer_b, peer_near, sibling)

    for n in range(list_sem.shape[0]):
        list_copy(n).wait()
        rows = []
        for i in range(n * part, (n + 1) * part):
            partial = None
            for j in range(columns):
                piece = lists_ref[i, :, j * LANES : (j + 1) * LANES].astype(jnp.float32)
                partial = piece * piece if partial is None else partial + piece * piece
            rows.append(0.5 * jnp.sum(partial.T, axis=0, keepdims=True))
        norms_ref[n * part : (n + 1) * part, :] = jnp.concatenate(rows, axis=0)

    relay(z, "a", sibling)
    relay(z, "b", sibling)
    relay(cross, "o", peer_near, sibling, peer_a, peer_b)
    send(peer_a, peer_b)

    batches = (
        ((z, "o"), (z, "x"), (z, "y"), (cross, "o")),
        ((cross, "x"), (cross, "y"), (opposite, "o"), (near, "o")),
        ((cross, "d"), (opposite, "x"), (opposite, "y"), (z, "d")),
        ((opposite, "d"), (near, "x"), (near, "y"), (near, "d")),
    )
    order = [
        number(p, *sides[side], core).astype(jnp.float32)
        for chips in batches
        for p, side in chips
        for core in range(2)
    ]
    target = jnp.where(lane8 < query_count, (stored >> 5).astype(jnp.float32), -1.0)
    mine = jnp.concatenate([jnp.where(target == d, 1.0, 0.0) for d in order], axis=0)
    rank = ranks(mine)
    spot = jnp.zeros(ids.shape, jnp.float32)
    for n, d in enumerate(order):
        spot = jnp.where(target == d, rank[n * 8 : (n + 1) * 8] + float(n * capacity), spot)
    wide = lax.broadcasted_iota(jnp.int32, (8, devices * capacity), 1).astype(jnp.float32)
    for q in range(0, query_count, 2):
        both = [jnp.where(spot[:, i : i + 1] == wide, 1.0, 0.0) for i in (q, q + 1)]
        place_ref[q * 8 : (q + 2) * 8, :] = jnp.concatenate(both, axis=0).astype(jnp.bfloat16)

    def back(target, block):
        return pltpu.make_async_remote_copy(
            src_ref=send_ref.at[target],
            dst_ref=got_ref.at[block],
            send_sem=back_send.at[target],
            recv_sem=back_recv.at[block],
            device_id=mesh_id(target),
            device_id_type=pl.DeviceIdType.MESH,
        )

    me_f = me.astype(jnp.float32)
    slots = 2 * CHIPS * capacity
    slot = lax.broadcasted_iota(jnp.int32, (capacity, LANES), 0).astype(jnp.float32)

    def both_of(place):
        p, side = place
        return pl.ds(number(p, *sides[side], 0), 2)

    def choose(chips):
        tables = [
            all_ref[both_of(chip), table_at:, :].astype(jnp.float32)[:, :8, :] for chip in chips
        ]
        tables = jnp.concatenate(tables, axis=0).reshape(2 * CHIPS * 8, LANES)
        lane = lax.broadcasted_iota(jnp.int32, tables.shape, 1)
        mine = jnp.where((lane < query_count) & (tables == me_f), 1.0, 0.0)
        rank = jnp.where(mine > 0.5, ranks(mine), -1.0)
        local = tables + 1.0
        at = (rank, pltpu.roll(rank, query_count, 1))
        what = (pltpu.roll(local, query_count, 1), local)
        picks, lists_of = [], []
        for t in range(2 * CHIPS):
            pick = jnp.zeros((capacity, LANES), jnp.float32)
            which = jnp.zeros((capacity, LANES), jnp.float32)
            for j in range(8):
                row = t * 8 + j
                hit = at[t % 2][row : row + 1, :] == slot
                pick = jnp.where(hit, 1.0, pick)
                which = jnp.where(hit, what[t % 2][row : row + 1, :], which)
            picks.append(pick.astype(jnp.bfloat16))
            lists_of.append(which)
        place = jnp.sum(jnp.concatenate(lists_of, axis=0), axis=1, keepdims=True)
        place = jnp.broadcast_to(place, (slots, LANES))
        return picks, place

    def select(chips, picks, picked):
        norm = jnp.zeros((slots, LANES), jnp.float32)
        for j in range(columns):
            rows = []
            for u, chip in enumerate(chips):
                pair = all_ref[
                    both_of(chip), j * query_count : (j + 1) * query_count, :
                ].reshape(2 * query_count, LANES)
                pick = jnp.concatenate(picks[2 * u : 2 * u + 2], axis=0)
                rows.append(jnp.dot(pick, pair, preferred_element_type=jnp.float32))
            piece = jnp.concatenate(rows, axis=0)
            norm = norm + piece * piece
            picked[:, j * LANES : (j + 1) * LANES] = piece.astype(jnp.bfloat16)
        return jnp.sum(norm, axis=1, keepdims=True)

    def encode(chips, best, norm):
        distance = jnp.maximum((norm - 2.0 * best) * (1.0 / width), 0.0)
        largest = jnp.maximum(jnp.max(distance, axis=1, keepdims=True), 1e-30)
        power = jnp.clip(jnp.ceil(jnp.log(largest) * LOG2E + 1e-3), -100.0, 120.0)
        code = jnp.clip(jnp.round(distance * (65535.0 * jnp.exp(power * -LN2))), 0.0, 65535.0)
        code = code.astype(jnp.int32)
        word = code[:, :LANES] | (code[:, LANES:] << 16)
        word = word.reshape(2 * CHIPS, capacity, LANES)
        whole = (2 * CHIPS, capacity, LANES)
        half = lax.broadcasted_iota(jnp.int32, whole, 0) // 2
        half = (half - 2 * (half // 2)) * 2 + c
        spot = lax.broadcasted_iota(jnp.int32, whole, 1) + half * capacity
        lane = lax.broadcasted_iota(jnp.int32, whole, 2)
        powers = jnp.broadcast_to(power, (slots, LANES)).reshape(whole)
        powers = jnp.sum(jnp.where(spot == lane, powers, 0.0), axis=1, keepdims=True)
        powers = powers.astype(jnp.int32)
        for u, chip in enumerate(chips):
            send_ref[both_of(chip), :capacity, :] = word[2 * u : 2 * u + 2]
            send_ref[both_of(chip), capacity : capacity + 1, :] = powers[2 * u : 2 * u + 2]

    returned = []

    def ends(p, side):
        own_chip = p is z and side == "o"
        return [twin_of(p, side)] if own_chip else [block_of(p, side), twin_of(p, side)]

    def give_back(chips):
        for p, side in chips:
            for block in ends(p, side):
                copy = back(block, me)
                copy.start()
                returned.append(copy)

    half = (
        (
            (cross, "a", peer_b, sibling),
            (cross, "b", sibling),
            (opposite, "o", sibling, peer_a, peer_b),
            (near, "o", sibling, peer_a, peer_b),
            (z, "d", sibling),
        ),
        (
            (cross, "d", sibling),
            (opposite, "a", sibling, peer_b),
            (opposite, "b", sibling),
        ),
        (),
        (),
    )
    late = ((), ((near, "a", peer_b, sibling), (near, "b", sibling)), (), ())
    soon = ((), (), ((opposite, "d", sibling), (near, "d", sibling)), ())
    picked_refs = (even_ref, odd_ref)

    def prepare(k):
        for p, side in batches[k]:
            arrived(twin_of(p, side))
        return choose(batches[k])

    def score(k, place, best, first, count):
        dots = lax.dot_general(
            picked_refs[k % 2][...],
            lists_ref[first : first + count].reshape(count * list_size, width),
            (((1,), (1,)), ((), ())),
            preferred_element_type=jnp.float32,
        )
        for i in range(count):
            n = first + i
            hit = place == n + 1.0
            hit = jnp.concatenate([hit] * (list_size // LANES), axis=1)
            value = dots[:, i * list_size : (i + 1) * list_size] - norms_ref[n : n + 1, :]
            best = jnp.where(hit, value, best)
        return best

    step = list_count // 4
    picks, place = prepare(0)
    norm = select(batches[0], picks, picked_refs[0])
    for k, chips in enumerate(batches):
        best = jnp.zeros((slots, list_size), jnp.float32)
        begin = 0
        for stop, relayed in ((1, soon[k]), (2, half[k]), (3, late[k])):
            if relayed or (stop == 3 and 0 < k < 3):
                best = score(k, place, best, begin * step, (stop - begin) * step)
                begin = stop
                for item in relayed:
                    relay(*item)
        ahead = 0 < k < len(batches) - 1
        if ahead:
            picks, later = prepare(k + 1)
        best = score(k, place, best, begin * step, (4 - begin) * step)
        if ahead:
            after = select(batches[k + 1], picks, picked_refs[(k + 1) % 2])
        encode(chips, best, norm)
        give_back(chips)
        if k == 0:
            picks, later = prepare(1)
            after = select(batches[1], picks, picked_refs[1])
        place, norm = later, after
    got_ref[me] = send_ref[me]

    def receive(chips):
        for p, side in chips:
            for block in ends(p, side):
                back(block, block).wait_recv()

    def unpack(some, k):
        codes, powers = [], []
        for chips in some:
            words = jnp.concatenate([got_ref[both_of(chip), :capacity, :] for chip in chips], axis=0)
            words = words.reshape(slots, LANES)
            pieces = [((words >> s) & 255).astype(jnp.float32) for s in (0, 8, 16, 24)]
            codes.append(jnp.concatenate([p.astype(jnp.bfloat16) for p in pieces], axis=1))
            for u in range(0, CHIPS, 2):
                rows = [
                    got_ref[both_of(chip), capacity : capacity + 1, :].astype(jnp.float32)
                    for chip in chips[u : u + 2]
                ]
                row = jnp.sum(jnp.concatenate(rows, axis=0), axis=0)
                powers.append(jnp.broadcast_to(row, (LANES, LANES)).astype(jnp.bfloat16))
        place = place_ref[:, k * slots : (k + len(some)) * slots]
        chosen = jnp.dot(
            place, jnp.concatenate(codes, axis=0), preferred_element_type=jnp.float32
        )
        power = lax.dot_general(
            place,
            jnp.concatenate(powers, axis=1),
            (((1,), (1,)), ((), ())),
            preferred_element_type=jnp.float32,
        )
        return jnp.concatenate([chosen, power], axis=1)

    for chips in batches[:-1]:
        receive(chips)
    total_ref[...] = unpack(batches[:-1], 0)
    receive(batches[-1])
    total = total_ref[...] + unpack(batches[-1:], len(batches) - 1)
    scale = jnp.exp(total[:, 4 * LANES :] * LN2) * (1.0 / 65535.0)
    for h in range(2):
        low = total[:, 2 * h * LANES : (2 * h + 1) * LANES]
        high = total[:, (2 * h + 1) * LANES : (2 * h + 2) * LANES]
        out_ref[:, h * LANES : (h + 1) * LANES] = (low + 256.0 * high) * scale
    result = pltpu.make_async_copy(out_ref, out_hbm, out_sem)
    result.start()
    for copy in sent:
        copy.wait_send()
    for copy in returned:
        copy.wait_send()
    result.wait()


def fused(queries, projection, lists, probes, owner_map):
    query_count, width = queries.shape
    probe_count = probes.shape[1]
    list_count, list_size = lists.shape[0], lists.shape[1]
    devices = PLANES * PLANE
    pairs, slots = query_count * probe_count, devices * CAPACITY
    rows = width // LANES * query_count + TABLE
    hbm = pl.BlockSpec(memory_space=pltpu.HBM)
    owners = owner_map.reshape(-1, LANES)
    words = (devices, CAPACITY + 1, LANES)
    scores = pl.pallas_call(
        fused_kernel,
        out_shape=jax.ShapeDtypeStruct((pairs, list_size), jnp.float32),
        in_specs=[hbm] * 5,
        out_specs=hbm,
        scratch_shapes=[
            pltpu.VMEM(queries.shape, jnp.bfloat16),
            pltpu.VMEM(projection.shape, jnp.bfloat16),
            pltpu.VMEM((probe_count, query_count), jnp.int32),
            pltpu.VMEM(owners.shape, jnp.int32),
            pltpu.VMEM((devices, rows, LANES), jnp.bfloat16),
            pltpu.VMEM(lists.shape, jnp.bfloat16),
            pltpu.VMEM((list_count, list_size), jnp.float32),
            pltpu.VMEM((2 * CHIPS * CAPACITY, width), jnp.bfloat16),
            pltpu.VMEM((2 * CHIPS * CAPACITY, width), jnp.bfloat16),
            pltpu.VMEM(words, jnp.int32),
            pltpu.VMEM(words, jnp.int32),
            pltpu.VMEM((pairs, slots), jnp.bfloat16),
            pltpu.VMEM((pairs, 5 * LANES), jnp.float32),
            pltpu.VMEM((pairs, list_size), jnp.float32),
            pltpu.SemaphoreType.DMA((4,)),
            pltpu.SemaphoreType.DMA((8,)),
            pltpu.SemaphoreType.DMA((devices,)),
            pltpu.SemaphoreType.DMA((devices,)),
            pltpu.SemaphoreType.DMA((devices,)),
            pltpu.SemaphoreType.DMA((devices,)),
            pltpu.SemaphoreType.DMA,
        ],
        compiler_params=pltpu.CompilerParams(
            collective_id=0, has_side_effects=True, vmem_limit_bytes=VMEM_LIMIT
        ),
    )(queries, projection, probes.T, owners, lists)
    return scores.reshape(query_count, probe_count, list_size)


def solution(mesh):
    placed = (
        P(AXES, None),
        P(),
        P(AXES, None, None),
        P(AXES, None),
        P(),
    )
    sizes = (mesh.shape["grp"], mesh.shape["own"])
    return jax.shard_map(
        fused if sizes == (8, 4) else general,
        mesh=mesh,
        in_specs=placed,
        out_specs=P(AXES, None, None),
        check_vma=False,
    )
```

```python
import jax
import jax.numpy as jnp
from jax import lax
from jax.experimental import pallas as pl
from jax.experimental.pallas import tpu as pltpu
from jax.sharding import PartitionSpec as P

AXES = ("grp", "own")
LANES = 128
LOG2E = 1.4426950408889634
LN2 = 0.6931471805599453


def select_kernel(queries, width, row_ref, all_ref, out_ref):
    devices = all_ref.shape[0]
    count = out_ref.shape[0]
    numbers = lax.broadcasted_iota(jnp.int32, (count, devices * queries), 1)
    pick = (numbers == row_ref[...]).astype(jnp.float32).astype(jnp.bfloat16)
    for j in range(width // LANES):
        part = all_ref[:, j * queries : (j + 1) * queries, :].reshape(devices * queries, LANES)
        out_ref[:, j * LANES : (j + 1) * LANES] = jnp.dot(
            pick, part, preferred_element_type=jnp.float32
        ).astype(jnp.bfloat16)


def select_rows(everyone, row_of, queries, width):
    slots = row_of.shape[0]
    block = min(256, slots)
    return pl.pallas_call(
        lambda *refs: select_kernel(queries, width, *refs),
        grid=(slots // block,),
        out_shape=jax.ShapeDtypeStruct((slots, width), jnp.bfloat16),
        in_specs=[
            pl.BlockSpec((block, 1), lambda i: (i, 0)),
            pl.BlockSpec(memory_space=pltpu.VMEM),
        ],
        out_specs=pl.BlockSpec((block, width), lambda i: (i, 0)),
        compiler_params=pltpu.CompilerParams(vmem_limit_bytes=48 * 2**20),
    )(row_of[:, None], everyone)


def score_kernel(blocks, rows_ref, lists_ref, spot_ref, out_ref, held):
    step = pl.program_id(0)
    count, list_size, width = lists_ref.shape
    capacity = rows_ref.shape[0] // count
    for n in range(count):
        rows = rows_ref[n * capacity : (n + 1) * capacity, :]
        dots = lax.dot_general(
            rows, lists_ref[n], (((1,), (1,)), ((), ())), preferred_element_type=jnp.float32
        )
        rows_f = rows.astype(jnp.float32)
        row_norm = jnp.sum(rows_f * rows_f, axis=1, keepdims=True)
        partial = None
        for j in range(width // LANES):
            part = lists_ref[n, :, j * LANES : (j + 1) * LANES].astype(jnp.float32)
            partial = part * part if partial is None else partial + part * part
        vec_norm = jnp.sum(partial.T, axis=0, keepdims=True)
        distance = jnp.maximum((row_norm + vec_norm - 2.0 * dots) / width, 0.0)
        largest = jnp.maximum(jnp.max(distance, axis=1, keepdims=True), 1e-30)
        power = jnp.clip(jnp.ceil(jnp.log(largest) * LOG2E + 1e-3), -100.0, 120.0)
        code = jnp.clip(jnp.round(distance * (65535.0 * jnp.exp(power * -LN2))), 0.0, 65535.0)
        high = jnp.floor(code * (1.0 / 256.0))
        low = code - high * 256.0
        place = pl.ds(pl.multiple_of((step * count + n) * capacity, 16), capacity)
        held[place, :list_size] = high.astype(jnp.bfloat16)
        held[place, list_size : 2 * list_size] = low.astype(jnp.bfloat16)
        held[place, 2 * list_size :] = jnp.broadcast_to(power, (capacity, LANES)).astype(
            jnp.bfloat16
        )

    @pl.when(step == pl.num_programs(0) - 1)
    def _():
        slots = held.shape[0]
        each = slots // blocks
        numbers = lax.broadcasted_iota(jnp.int32, (slots, slots), 1)
        pick = (numbers == spot_ref[...]).astype(jnp.float32).astype(jnp.bfloat16)
        got = jnp.dot(pick, held[...], preferred_element_type=jnp.float32)
        code = got[:, :list_size] * 256.0 + got[:, list_size : 2 * list_size] - 32768.0
        parts = [
            code[:, h * LANES : (h + 1) * LANES].reshape(blocks, each, LANES)
            for h in range(list_size // LANES)
        ]
        powers = got[:, 2 * list_size :].reshape(blocks, each, LANES)
        slot = lax.broadcasted_iota(jnp.int32, powers.shape, 1)
        lane = lax.broadcasted_iota(jnp.int32, powers.shape, 2)
        powers = jnp.sum(jnp.where(slot == lane, powers, 0.0), axis=1, keepdims=True)
        parts.append(jnp.broadcast_to(powers, (blocks, 16, LANES)))
        whole = jnp.concatenate(parts, axis=1)
        out_ref[...] = whole.astype(jnp.int32).astype(jnp.int16)


def score(grouped, lists, spot, blocks):
    list_count, list_size, width = lists.shape
    slots = grouped.shape[0]
    count = 4
    out_rows = (slots // blocks) * list_size // LANES + 16
    return pl.pallas_call(
        lambda *refs: score_kernel(blocks, *refs),
        grid=(list_count // count,),
        out_shape=jax.ShapeDtypeStruct((blocks, out_rows, LANES), jnp.int16),
        in_specs=[
            pl.BlockSpec((slots // list_count * count, width), lambda i: (i, 0)),
            pl.BlockSpec((count, list_size, width), lambda i: (i, 0, 0)),
            pl.BlockSpec((slots, 1), lambda i: (0, 0)),
        ],
        out_specs=pl.BlockSpec((blocks, out_rows, LANES), lambda i: (0, 0, 0)),
        scratch_shapes=[pltpu.VMEM((slots, 2 * list_size + LANES), jnp.bfloat16)],
        compiler_params=pltpu.CompilerParams(vmem_limit_bytes=40 * 2**20),
    )(grouped, lists, spot[:, None])


def exchange_kernel(device_count, owner_count, out_ref, in_ref, send_sem, recv_sem):
    me = lax.axis_index("grp") * owner_count + lax.axis_index("own")

    def at(k):
        other = lax.rem(me + k, device_count)
        return other, (other // owner_count, lax.rem(other, owner_count))

    barrier = pltpu.get_barrier_semaphore()

    @pl.loop(1, device_count)
    def _(k):
        pl.semaphore_signal(
            barrier, inc=1, device_id=at(k)[1], device_id_type=pl.DeviceIdType.MESH
        )

    pl.semaphore_wait(barrier, device_count - 1)

    def describe(k, block):
        other, where = at(k)
        return pltpu.make_async_remote_copy(
            src_ref=out_ref.at[other],
            dst_ref=in_ref.at[block],
            send_sem=send_sem.at[k],
            recv_sem=recv_sem.at[block],
            device_id=where,
            device_id_type=pl.DeviceIdType.MESH,
        )

    @pl.loop(1, device_count)
    def _(k):
        describe(k, me).start()

    in_ref[me] = out_ref[me]

    @pl.loop(1, device_count)
    def _(k):
        describe(k, at(k)[0]).wait_recv()

    @pl.loop(1, device_count)
    def _(k):
        describe(k, me).wait_send()


def exchange(blocks):
    owner_count = lax.axis_size("own")
    device_count = blocks.shape[0]
    return pl.pallas_call(
        lambda *refs: exchange_kernel(device_count, owner_count, *refs),
        out_shape=jax.ShapeDtypeStruct(blocks.shape, blocks.dtype),
        in_specs=[pl.BlockSpec(memory_space=pltpu.VMEM)],
        out_specs=pl.BlockSpec(memory_space=pltpu.VMEM),
        scratch_shapes=[
            pltpu.SemaphoreType.DMA((device_count,)),
            pltpu.SemaphoreType.DMA((device_count,)),
        ],
        compiler_params=pltpu.CompilerParams(
            collective_id=1, has_side_effects=True, vmem_limit_bytes=16 * 2**20
        ),
    )(blocks)


def general(queries, projection, lists, probes, owner_map):
    query_count, width = queries.shape
    probe_count = probes.shape[1]
    lists_here, list_size = lists.shape[0], lists.shape[1]
    device_count = lax.axis_size("grp") * lax.axis_size("own")
    pairs = query_count * probe_count
    capacity = 2 * pairs // device_count
    list_capacity = device_count * capacity // lists_here
    slots = device_count * capacity
    me = lax.axis_index(AXES)

    projected = jnp.dot(queries, projection, preferred_element_type=jnp.float32).astype(
        jnp.bfloat16
    )
    stored = jnp.take(owner_map, probes.reshape(-1))
    target = stored // lists_here
    local = stored % lists_here
    to_target = (target[:, None] == jnp.arange(device_count, dtype=jnp.int32)[None, :]).astype(
        jnp.bfloat16
    )
    step = jnp.arange(pairs, dtype=jnp.int32)
    earlier = (step[None, :] < step[:, None]).astype(jnp.bfloat16)
    before = jnp.dot(earlier, to_target, preferred_element_type=jnp.float32)
    rank = jnp.sum(before * to_target.astype(jnp.float32), axis=1).astype(jnp.int32)
    position = target * capacity + rank

    at_rank = (rank[:, None] == jnp.arange(capacity, dtype=jnp.int32)[None, :]).astype(jnp.bfloat16)
    query_of = step // probe_count
    what = jnp.stack([jnp.ones_like(step), query_of, local], axis=0).astype(jnp.bfloat16)
    weighted = to_target.T[None] * what[:, None, :]
    table = jnp.dot(
        weighted.reshape(3 * device_count, pairs), at_rank, preferred_element_type=jnp.float32
    ).reshape(3, device_count, capacity)
    table = jnp.where(table[:1] > 0.5, table[1:], -1.0).astype(jnp.bfloat16)
    columns = width // LANES
    extra = -(-(2 * slots) // (16 * LANES)) * 16
    table = jnp.pad(table.reshape(-1), (0, extra * LANES - 2 * slots)).reshape(extra, LANES)
    stacked = projected.reshape(query_count, columns, LANES).transpose(1, 0, 2)
    stacked = stacked.reshape(columns * query_count, LANES)

    everyone = lax.all_gather(jnp.concatenate([stacked, table], axis=0), AXES, tiled=False)
    tables = everyone[:, columns * query_count :].reshape(device_count, -1)[:, : 2 * slots]
    tables = tables.reshape(device_count, 2, device_count, capacity)
    mine = lax.dynamic_index_in_dim(tables, me, axis=2, keepdims=False).astype(jnp.int32)
    asked_query = mine[:, 0].reshape(-1)
    asked_list = mine[:, 1].reshape(-1)
    row_of = (
        asked_query + query_count * (jnp.arange(slots, dtype=jnp.int32) // capacity)
    )

    in_list = (asked_list[:, None] == jnp.arange(lists_here, dtype=jnp.int32)[None, :]).astype(
        jnp.bfloat16
    )
    place = jnp.arange(slots, dtype=jnp.int32)
    earlier = (place[None, :] < place[:, None]).astype(jnp.bfloat16)
    before = jnp.dot(earlier, in_list, preferred_element_type=jnp.float32)
    order = jnp.sum(before * in_list.astype(jnp.float32), axis=1).astype(jnp.int32)
    valid = asked_list >= 0
    spot = jnp.where(valid, asked_list * list_capacity + order, -1)
    hit = spot[:, None] == jnp.arange(lists_here * list_capacity, dtype=jnp.int32)[None, :]
    grouped_row = jnp.sum(jnp.where(hit, row_of[:, None], 0), axis=0)
    grouped = select_rows(everyone, grouped_row, query_count, width)
    blocks = score(grouped, lists, spot, device_count)
    answer_rows = capacity * list_size // LANES
    got = exchange(blocks).astype(jnp.float32)
    powers = got[:, answer_rows:].reshape(device_count, -1)[:, :capacity].reshape(slots, 1)
    returned = (
        got[:, :answer_rows]
        .reshape(device_count, list_size // LANES, capacity, LANES)
        .transpose(0, 2, 1, 3)
        .reshape(slots, list_size)
    )
    returned = (returned + 32768.0) * (jnp.exp2(powers) / 65535.0)
    return returned[position].reshape(query_count, probe_count, list_size)


PLANES = 4
PLANE = 8
TABLE = 16
BATCH = 8
CAPACITY = 32
VMEM_LIMIT = 56 * 2**20


def number(z, x, y, c):
    return z * PLANE + x * 4 + y * 2 + c


def mesh_id(n):
    return (n // 4, lax.rem(n, 4))


def ranks(mine):
    lane = lax.broadcasted_iota(jnp.int32, mine.shape, 1)
    within = mine
    for reach in (1, 2, 4, 8, 16, 32, 64):
        within = within + jnp.where(lane >= reach, pltpu.roll(within, reach, 1), 0.0)
    totals = jnp.broadcast_to(within[:, LANES - 1 :], mine.shape).reshape(-1, 8, LANES)
    probe = lax.broadcasted_iota(jnp.int32, totals.shape, 1)
    before = totals
    for reach in (1, 2, 4):
        before = before + jnp.where(probe >= reach, pltpu.roll(before, reach, 1), 0.0)
    return within - mine + (before - totals).reshape(mine.shape)


def fused_kernel(
    queries_hbm,
    projection_hbm,
    probes_hbm,
    owner_hbm,
    lists_hbm,
    out_hbm,
    queries_ref,
    projection_ref,
    probes_ref,
    owner_ref,
    all_ref,
    lists_ref,
    norms_ref,
    even_ref,
    odd_ref,
    send_ref,
    got_ref,
    place_ref,
    total_ref,
    out_ref,
    input_sem,
    list_sem,
    spread_send,
    spread_recv,
    back_send,
    back_recv,
    out_sem,
):
    grp, own = lax.axis_index("grp"), lax.axis_index("own")
    z, x, y, c = grp // 2, lax.rem(grp, 2), own // 2, lax.rem(own, 2)
    me = number(z, x, y, c)
    devices = all_ref.shape[0]
    query_count, width = queries_ref.shape
    list_count, list_size = lists_ref.shape[0], lists_ref.shape[1]
    columns = width // LANES
    table_at = columns * query_count
    capacity = CAPACITY

    inputs = [
        pltpu.make_async_copy(src, dst, input_sem.at[i])
        for i, (src, dst) in enumerate(
            (
                (projection_hbm, projection_ref),
                (queries_hbm, queries_ref),
                (probes_hbm, probes_ref),
                (owner_hbm, owner_ref),
            )
        )
    ]
    for copy in inputs:
        copy.start()
    barrier = pltpu.get_barrier_semaphore()

    near, cross, opposite = z + 1 - 2 * lax.rem(z, 2), lax.rem(z + 2, PLANES), PLANES - 1 - z
    xa, ya = x * c + (1 - x) * (1 - c), y * (1 - c) + (1 - y) * c
    xb, yb = x * (1 - c) + (1 - x) * c, y * c + (1 - y) * (1 - c)
    sides = {"o": (x, y), "a": (xa, ya), "b": (xb, yb), "d": (1 - x, 1 - y)}
    sides |= {"x": (1 - x, y), "y": (x, 1 - y)}

    def block_of(p, side, twin=False):
        return number(p, *sides[side], 1 - c if twin else c)

    peer_a, peer_b = block_of(z, "a"), block_of(z, "b")
    peer_near, peer_cross = block_of(near, "o"), block_of(cross, "o")
    sibling = block_of(z, "o", True)
    peers = (peer_cross, peer_a, peer_b, peer_near, sibling)
    for peer in peers:
        pl.semaphore_signal(
            barrier, inc=1, device_id=mesh_id(peer), device_id_type=pl.DeviceIdType.MESH
        )

    part = list_count // list_sem.shape[0]

    def list_copy(n):
        piece = pl.ds(n * part, part)
        return pltpu.make_async_copy(lists_hbm.at[piece], lists_ref.at[piece], list_sem.at[n])

    for n in range(list_sem.shape[0]):
        list_copy(n).start()
    for copy in inputs:
        copy.wait()

    projected = jnp.dot(
        queries_ref[...], projection_ref[...], preferred_element_type=jnp.float32
    ).astype(jnp.bfloat16)
    for j in range(columns):
        all_ref[me, j * query_count : (j + 1) * query_count, :] = projected[
            :, j * LANES : (j + 1) * LANES
        ]
    ids = jnp.concatenate([probes_ref[...], probes_ref[...]], axis=1)
    low, high = ids & (LANES - 1), ids >> 7
    stored = jnp.zeros_like(ids)
    for h in range(owner_ref.shape[0]):
        row = jnp.broadcast_to(owner_ref[h : h + 1, :], ids.shape)
        found = jnp.take_along_axis(row, low, axis=1, mode="promise_in_bounds")
        stored = jnp.where(high == h, found, stored)
    lane8 = lax.broadcasted_iota(jnp.int32, ids.shape, 1)
    table = jnp.where(lane8 < query_count, stored >> 5, stored & 31).astype(jnp.float32)
    all_ref[me, table_at:, :] = jnp.concatenate([table, jnp.zeros_like(table)], axis=0).astype(
        jnp.bfloat16
    )
    pl.semaphore_wait(barrier, len(peers))

    sent = []

    def describe(block, peer, slot):
        return pltpu.make_async_remote_copy(
            src_ref=all_ref.at[block],
            dst_ref=all_ref.at[block],
            send_sem=spread_send.at[slot],
            recv_sem=spread_recv.at[block],
            device_id=mesh_id(peer),
            device_id_type=pl.DeviceIdType.MESH,
        )

    def send(block, *peers):
        for peer in peers:
            copy = describe(block, peer, len(sent))
            copy.start()
            sent.append(copy)

    def arrived(block):
        describe(block, sibling, 0).wait_recv()

    def relay(p, side, *peers):
        arrived(block_of(p, side))
        send(block_of(p, side), *peers)

    send(me, *peers)

    for n in range(list_sem.shape[0]):
        list_copy(n).wait()
        rows = []
        for i in range(n * part, (n + 1) * part):
            partial = None
            for j in range(columns):
                piece = lists_ref[i, :, j * LANES : (j + 1) * LANES].astype(jnp.float32)
                partial = piece * piece if partial is None else partial + piece * piece
            rows.append(0.5 * jnp.sum(partial.T, axis=0, keepdims=True))
        norms_ref[n * part : (n + 1) * part, :] = jnp.concatenate(rows, axis=0)

    relay(z, "a", sibling)
    relay(z, "b", sibling)
    relay(cross, "o", peer_a, peer_b, sibling, peer_near)
    send(peer_a, peer_b)

    itself = (z, "o")
    batches = (
        (
            itself,
            (z, "o", True),
            (z, "x"),
            (z, "x", True),
            (z, "y"),
            (z, "y", True),
            (cross, "o"),
            (cross, "o", True),
        ),
        (
            (cross, "x"),
            (cross, "x", True),
            (cross, "y"),
            (cross, "y", True),
            (opposite, "o"),
            (opposite, "o", True),
            (near, "o"),
            (near, "o", True),
        ),
        (
            (cross, "d"),
            (cross, "d", True),
            (opposite, "x"),
            (opposite, "x", True),
            (opposite, "y"),
            (opposite, "y", True),
            (z, "d"),
            (near, "x"),
        ),
        (
            (opposite, "d"),
            (opposite, "d", True),
            (z, "d", True),
            (near, "x", True),
            (near, "y"),
            (near, "y", True),
            (near, "d"),
            (near, "d", True),
        ),
    )
    order = [block_of(*where).astype(jnp.float32) for chips in batches for where in chips]
    target = jnp.where(lane8 < query_count, (stored >> 5).astype(jnp.float32), -1.0)
    mine = jnp.concatenate([jnp.where(target == d, 1.0, 0.0) for d in order], axis=0)
    rank = ranks(mine)
    spot = jnp.zeros(ids.shape, jnp.float32)
    for n, d in enumerate(order):
        spot = jnp.where(target == d, rank[n * 8 : (n + 1) * 8] + float(n * capacity), spot)
    wide = lax.broadcasted_iota(jnp.int32, (8, devices * capacity), 1).astype(jnp.float32)
    for q in range(0, query_count, 2):
        both = [jnp.where(spot[:, i : i + 1] == wide, 1.0, 0.0) for i in (q, q + 1)]
        place_ref[q * 8 : (q + 2) * 8, :] = jnp.concatenate(both, axis=0).astype(jnp.bfloat16)

    def back(n):
        return pltpu.make_async_remote_copy(
            src_ref=send_ref.at[n],
            dst_ref=got_ref.at[n],
            send_sem=back_send.at[n],
            recv_sem=back_recv.at[n],
            device_id=mesh_id(block_of(*batches[n // BATCH][n % BATCH])),
            device_id_type=pl.DeviceIdType.MESH,
        )

    me_f = me.astype(jnp.float32)
    slots = BATCH * capacity
    slot = lax.broadcasted_iota(jnp.int32, (capacity, LANES), 0).astype(jnp.float32)

    def choose(chips):
        tables = [
            all_ref[block_of(*where), table_at:, :].astype(jnp.float32)[:8, :] for where in chips
        ]
        tables = jnp.concatenate(tables, axis=0)
        lane = lax.broadcasted_iota(jnp.int32, tables.shape, 1)
        mine = jnp.where((lane < query_count) & (tables == me_f), 1.0, 0.0)
        rank = jnp.where(mine > 0.5, ranks(mine), -1.0)
        local = tables + 1.0
        at = (rank, pltpu.roll(rank, query_count, 1))
        what = (pltpu.roll(local, query_count, 1), local)
        picks, lists_of = [], []
        for t in range(BATCH):
            pick = jnp.zeros((capacity, LANES), jnp.float32)
            which = jnp.zeros((capacity, LANES), jnp.float32)
            for j in range(8):
                row = t * 8 + j
                hit = at[t % 2][row : row + 1, :] == slot
                pick = jnp.where(hit, 1.0, pick)
                which = jnp.where(hit, what[t % 2][row : row + 1, :], which)
            picks.append(pick.astype(jnp.bfloat16))
            lists_of.append(which)
        place = jnp.sum(jnp.concatenate(lists_of, axis=0), axis=1, keepdims=True)
        place = jnp.broadcast_to(place, (slots, LANES))
        return picks, place

    def select(chips, picks, picked):
        norm = jnp.zeros((slots, LANES), jnp.float32)
        for j in range(columns):
            rows = []
            for u in range(0, BATCH, 2):
                pair = [
                    all_ref[block_of(*where), j * query_count : (j + 1) * query_count, :]
                    for where in chips[u : u + 2]
                ]
                pair = jnp.concatenate(pair, axis=0)
                pick = jnp.concatenate(picks[u : u + 2], axis=0)
                rows.append(jnp.dot(pick, pair, preferred_element_type=jnp.float32))
            piece = jnp.concatenate(rows, axis=0)
            norm = norm + piece * piece
            picked[:, j * LANES : (j + 1) * LANES] = piece.astype(jnp.bfloat16)
        return jnp.sum(norm, axis=1, keepdims=True)

    def encode(k, best, norm):
        distance = jnp.maximum((norm - 2.0 * best) * (1.0 / width), 0.0)
        largest = jnp.maximum(jnp.max(distance, axis=1, keepdims=True), 1e-30)
        power = jnp.clip(jnp.ceil(jnp.log(largest) * LOG2E + 1e-3), -100.0, 120.0)
        code = jnp.clip(jnp.round(distance * (65535.0 * jnp.exp(power * -LN2))), 0.0, 65535.0)
        code = code.astype(jnp.int32)
        word = code[:, :LANES] | (code[:, LANES:] << 16)
        whole = (BATCH, capacity, LANES)
        word = word.reshape(whole)
        quarter = lax.broadcasted_iota(jnp.int32, whole, 0) & 3
        spot = lax.broadcasted_iota(jnp.int32, whole, 1) + quarter * capacity
        lane = lax.broadcasted_iota(jnp.int32, whole, 2)
        powers = jnp.broadcast_to(power, (slots, LANES)).reshape(whole)
        powers = jnp.sum(jnp.where(spot == lane, powers, 0.0), axis=1, keepdims=True)
        powers = powers.astype(jnp.int32)
        send_ref[k * BATCH : (k + 1) * BATCH, :capacity, :] = word
        send_ref[k * BATCH : (k + 1) * BATCH, capacity : capacity + 1, :] = powers

    returned = []

    def others(k):
        return [back(n) for n in range(max(k * BATCH, 1), (k + 1) * BATCH)]

    def give_back(k):
        for copy in others(k):
            copy.start()
            returned.append(copy)

    relays = {
        (0, 3): (
            (cross, "a", peer_b, sibling),
            (cross, "b", sibling),
            (opposite, "o", peer_a, peer_b, sibling),
            (z, "d", peer_near, sibling),
        ),
        (1, 2): (
            (cross, "d", peer_near, sibling),
            (opposite, "a", sibling),
            (opposite, "b", sibling),
            (near, "a", sibling),
            (near, "b", sibling),
        ),
        (2, 1): ((near, "d", sibling), (opposite, "d", sibling)),
    }
    picked_refs = (even_ref, odd_ref)

    def prepare(k):
        for where in batches[k]:
            if len(where) == 3:
                arrived(block_of(*where))
        return choose(batches[k])

    def score(k, place, best, first, count):
        dots = lax.dot_general(
            picked_refs[k % 2][...],
            lists_ref[first : first + count].reshape(count * list_size, width),
            (((1,), (1,)), ((), ())),
            preferred_element_type=jnp.float32,
        )
        for i in range(count):
            n = first + i
            hit = place == n + 1.0
            hit = jnp.concatenate([hit] * (list_size // LANES), axis=1)
            value = dots[:, i * list_size : (i + 1) * list_size] - norms_ref[n : n + 1, :]
            best = jnp.where(hit, value, best)
        return best

    step = list_count // 4
    for where in batches[0]:
        if len(where) == 3:
            arrived(block_of(*where))
    relay(near, "o", peer_a, peer_b, sibling)
    picks, place = choose(batches[0])
    norm = select(batches[0], picks, picked_refs[0])
    for k, chips in enumerate(batches):
        best = jnp.zeros((slots, list_size), jnp.float32)
        begin = 0
        for stop in (1, 2, 3):
            relayed = relays.get((k, stop), ())
            if relayed or (stop == 3 and 0 < k < 3):
                best = score(k, place, best, begin * step, (stop - begin) * step)
                begin = stop
                for item in relayed:
                    relay(*item)
        ahead = 0 < k < len(batches) - 1
        if ahead:
            picks, later = prepare(k + 1)
        best = score(k, place, best, begin * step, (4 - begin) * step)
        if ahead:
            after = select(batches[k + 1], picks, picked_refs[(k + 1) % 2])
        encode(k, best, norm)
        give_back(k)
        if k == 0:
            picks, later = prepare(1)
            after = select(batches[1], picks, picked_refs[1])
        place, norm = later, after
    got_ref[0] = send_ref[0]

    def receive(k):
        for copy in others(k):
            copy.wait_recv()

    def unpack(k, count):
        mine = slice(k * BATCH, (k + count) * BATCH)
        words = got_ref[mine, :capacity, :].reshape(count * slots, LANES)
        codes = [((words >> s) & 255).astype(jnp.float32) for s in (0, 8, 16, 24)]
        codes = jnp.concatenate([p.astype(jnp.bfloat16) for p in codes], axis=1)
        powers = got_ref[mine, capacity : capacity + 1, :].astype(jnp.float32)
        powers = jnp.sum(powers.reshape(count * BATCH // 4, 4, LANES), axis=1)
        powers = jnp.concatenate(
            [jnp.broadcast_to(powers[g : g + 1], (LANES, LANES)) for g in range(powers.shape[0])],
            axis=1,
        ).astype(jnp.bfloat16)
        place = place_ref[:, k * slots : (k + count) * slots]
        chosen = jnp.dot(place, codes, preferred_element_type=jnp.float32)
        power = lax.dot_general(
            place,
            powers,
            (((1,), (1,)), ((), ())),
            preferred_element_type=jnp.float32,
        )
        return jnp.concatenate([chosen, power], axis=1)

    for k in range(len(batches) - 1):
        receive(k)
    total_ref[...] = unpack(0, len(batches) - 1)
    receive(len(batches) - 1)
    total = total_ref[...] + unpack(len(batches) - 1, 1)
    scale = jnp.exp(total[:, 4 * LANES :] * LN2) * (1.0 / 65535.0)
    for h in range(2):
        low = total[:, 2 * h * LANES : (2 * h + 1) * LANES]
        high = total[:, (2 * h + 1) * LANES : (2 * h + 2) * LANES]
        out_ref[:, h * LANES : (h + 1) * LANES] = (low + 256.0 * high) * scale
    result = pltpu.make_async_copy(out_ref, out_hbm, out_sem)
    result.start()
    for copy in sent:
        copy.wait_send()
    for copy in returned:
        copy.wait_send()
    result.wait()


def fused(queries, projection, lists, probes, owner_map):
    query_count, width = queries.shape
    probe_count = probes.shape[1]
    list_count, list_size = lists.shape[0], lists.shape[1]
    devices = PLANES * PLANE
    pairs, slots = query_count * probe_count, devices * CAPACITY
    rows = width // LANES * query_count + TABLE
    hbm = pl.BlockSpec(memory_space=pltpu.HBM)
    owners = owner_map.reshape(-1, LANES)
    words = (devices, CAPACITY + 1, LANES)
    scores = pl.pallas_call(
        fused_kernel,
        out_shape=jax.ShapeDtypeStruct((pairs, list_size), jnp.float32),
        in_specs=[hbm] * 5,
        out_specs=hbm,
        scratch_shapes=[
            pltpu.VMEM(queries.shape, jnp.bfloat16),
            pltpu.VMEM(projection.shape, jnp.bfloat16),
            pltpu.VMEM((probe_count, query_count), jnp.int32),
            pltpu.VMEM(owners.shape, jnp.int32),
            pltpu.VMEM((devices, rows, LANES), jnp.bfloat16),
            pltpu.VMEM(lists.shape, jnp.bfloat16),
            pltpu.VMEM((list_count, list_size), jnp.float32),
            pltpu.VMEM((BATCH * CAPACITY, width), jnp.bfloat16),
            pltpu.VMEM((BATCH * CAPACITY, width), jnp.bfloat16),
            pltpu.VMEM(words, jnp.int32),
            pltpu.VMEM(words, jnp.int32),
            pltpu.VMEM((pairs, slots), jnp.bfloat16),
            pltpu.VMEM((pairs, 5 * LANES), jnp.float32),
            pltpu.VMEM((pairs, list_size), jnp.float32),
            pltpu.SemaphoreType.DMA((4,)),
            pltpu.SemaphoreType.DMA((8,)),
            pltpu.SemaphoreType.DMA((devices,)),
            pltpu.SemaphoreType.DMA((devices,)),
            pltpu.SemaphoreType.DMA((devices,)),
            pltpu.SemaphoreType.DMA((devices,)),
            pltpu.SemaphoreType.DMA,
        ],
        compiler_params=pltpu.CompilerParams(
            collective_id=0, has_side_effects=True, vmem_limit_bytes=VMEM_LIMIT
        ),
    )(queries, projection, probes.T, owners, lists)
    return scores.reshape(query_count, probe_count, list_size)


def solution(mesh):
    placed = (
        P(AXES, None),
        P(),
        P(AXES, None, None),
        P(AXES, None),
        P(),
    )
    sizes = (mesh.shape["grp"], mesh.shape["own"])
    return jax.shard_map(
        fused if sizes == (8, 4) else general,
        mesh=mesh,
        in_specs=placed,
        out_specs=P(AXES, None, None),
        check_vma=False,
    )
```

```python
import jax
import jax.numpy as jnp
from jax import lax
from jax.experimental import pallas as pl
from jax.experimental.pallas import tpu as pltpu
from jax.sharding import PartitionSpec as P

AXES = ("grp", "own")
LANES = 128
LOG2E = 1.4426950408889634
LN2 = 0.6931471805599453


def select_kernel(queries, width, row_ref, all_ref, out_ref):
    devices = all_ref.shape[0]
    count = out_ref.shape[0]
    numbers = lax.broadcasted_iota(jnp.int32, (count, devices * queries), 1)
    pick = (numbers == row_ref[...]).astype(jnp.float32).astype(jnp.bfloat16)
    for j in range(width // LANES):
        part = all_ref[:, j * queries : (j + 1) * queries, :].reshape(devices * queries, LANES)
        out_ref[:, j * LANES : (j + 1) * LANES] = jnp.dot(
            pick, part, preferred_element_type=jnp.float32
        ).astype(jnp.bfloat16)


def select_rows(everyone, row_of, queries, width):
    slots = row_of.shape[0]
    block = min(256, slots)
    return pl.pallas_call(
        lambda *refs: select_kernel(queries, width, *refs),
        grid=(slots // block,),
        out_shape=jax.ShapeDtypeStruct((slots, width), jnp.bfloat16),
        in_specs=[
            pl.BlockSpec((block, 1), lambda i: (i, 0)),
            pl.BlockSpec(memory_space=pltpu.VMEM),
        ],
        out_specs=pl.BlockSpec((block, width), lambda i: (i, 0)),
        compiler_params=pltpu.CompilerParams(vmem_limit_bytes=48 * 2**20),
    )(row_of[:, None], everyone)


def score_kernel(blocks, rows_ref, lists_ref, spot_ref, out_ref, held):
    step = pl.program_id(0)
    count, list_size, width = lists_ref.shape
    capacity = rows_ref.shape[0] // count
    for n in range(count):
        rows = rows_ref[n * capacity : (n + 1) * capacity, :]
        dots = lax.dot_general(
            rows, lists_ref[n], (((1,), (1,)), ((), ())), preferred_element_type=jnp.float32
        )
        rows_f = rows.astype(jnp.float32)
        row_norm = jnp.sum(rows_f * rows_f, axis=1, keepdims=True)
        partial = None
        for j in range(width // LANES):
            part = lists_ref[n, :, j * LANES : (j + 1) * LANES].astype(jnp.float32)
            partial = part * part if partial is None else partial + part * part
        vec_norm = jnp.sum(partial.T, axis=0, keepdims=True)
        distance = jnp.maximum((row_norm + vec_norm - 2.0 * dots) / width, 0.0)
        largest = jnp.maximum(jnp.max(distance, axis=1, keepdims=True), 1e-30)
        power = jnp.clip(jnp.ceil(jnp.log(largest) * LOG2E + 1e-3), -100.0, 120.0)
        code = jnp.clip(jnp.round(distance * (65535.0 * jnp.exp(power * -LN2))), 0.0, 65535.0)
        high = jnp.floor(code * (1.0 / 256.0))
        low = code - high * 256.0
        place = pl.ds(pl.multiple_of((step * count + n) * capacity, 16), capacity)
        held[place, :list_size] = high.astype(jnp.bfloat16)
        held[place, list_size : 2 * list_size] = low.astype(jnp.bfloat16)
        held[place, 2 * list_size :] = jnp.broadcast_to(power, (capacity, LANES)).astype(
            jnp.bfloat16
        )

    @pl.when(step == pl.num_programs(0) - 1)
    def _():
        slots = held.shape[0]
        each = slots // blocks
        numbers = lax.broadcasted_iota(jnp.int32, (slots, slots), 1)
        pick = (numbers == spot_ref[...]).astype(jnp.float32).astype(jnp.bfloat16)
        got = jnp.dot(pick, held[...], preferred_element_type=jnp.float32)
        code = got[:, :list_size] * 256.0 + got[:, list_size : 2 * list_size] - 32768.0
        parts = [
            code[:, h * LANES : (h + 1) * LANES].reshape(blocks, each, LANES)
            for h in range(list_size // LANES)
        ]
        powers = got[:, 2 * list_size :].reshape(blocks, each, LANES)
        slot = lax.broadcasted_iota(jnp.int32, powers.shape, 1)
        lane = lax.broadcasted_iota(jnp.int32, powers.shape, 2)
        powers = jnp.sum(jnp.where(slot == lane, powers, 0.0), axis=1, keepdims=True)
        parts.append(jnp.broadcast_to(powers, (blocks, 16, LANES)))
        whole = jnp.concatenate(parts, axis=1)
        out_ref[...] = whole.astype(jnp.int32).astype(jnp.int16)


def score(grouped, lists, spot, blocks):
    list_count, list_size, width = lists.shape
    slots = grouped.shape[0]
    count = 4
    out_rows = (slots // blocks) * list_size // LANES + 16
    return pl.pallas_call(
        lambda *refs: score_kernel(blocks, *refs),
        grid=(list_count // count,),
        out_shape=jax.ShapeDtypeStruct((blocks, out_rows, LANES), jnp.int16),
        in_specs=[
            pl.BlockSpec((slots // list_count * count, width), lambda i: (i, 0)),
            pl.BlockSpec((count, list_size, width), lambda i: (i, 0, 0)),
            pl.BlockSpec((slots, 1), lambda i: (0, 0)),
        ],
        out_specs=pl.BlockSpec((blocks, out_rows, LANES), lambda i: (0, 0, 0)),
        scratch_shapes=[pltpu.VMEM((slots, 2 * list_size + LANES), jnp.bfloat16)],
        compiler_params=pltpu.CompilerParams(vmem_limit_bytes=40 * 2**20),
    )(grouped, lists, spot[:, None])


def exchange_kernel(device_count, owner_count, out_ref, in_ref, send_sem, recv_sem):
    me = lax.axis_index("grp") * owner_count + lax.axis_index("own")

    def at(k):
        other = lax.rem(me + k, device_count)
        return other, (other // owner_count, lax.rem(other, owner_count))

    barrier = pltpu.get_barrier_semaphore()

    @pl.loop(1, device_count)
    def _(k):
        pl.semaphore_signal(
            barrier, inc=1, device_id=at(k)[1], device_id_type=pl.DeviceIdType.MESH
        )

    pl.semaphore_wait(barrier, device_count - 1)

    def describe(k, block):
        other, where = at(k)
        return pltpu.make_async_remote_copy(
            src_ref=out_ref.at[other],
            dst_ref=in_ref.at[block],
            send_sem=send_sem.at[k],
            recv_sem=recv_sem.at[block],
            device_id=where,
            device_id_type=pl.DeviceIdType.MESH,
        )

    @pl.loop(1, device_count)
    def _(k):
        describe(k, me).start()

    in_ref[me] = out_ref[me]

    @pl.loop(1, device_count)
    def _(k):
        describe(k, at(k)[0]).wait_recv()

    @pl.loop(1, device_count)
    def _(k):
        describe(k, me).wait_send()


def exchange(blocks):
    owner_count = lax.axis_size("own")
    device_count = blocks.shape[0]
    return pl.pallas_call(
        lambda *refs: exchange_kernel(device_count, owner_count, *refs),
        out_shape=jax.ShapeDtypeStruct(blocks.shape, blocks.dtype),
        in_specs=[pl.BlockSpec(memory_space=pltpu.VMEM)],
        out_specs=pl.BlockSpec(memory_space=pltpu.VMEM),
        scratch_shapes=[
            pltpu.SemaphoreType.DMA((device_count,)),
            pltpu.SemaphoreType.DMA((device_count,)),
        ],
        compiler_params=pltpu.CompilerParams(
            collective_id=1, has_side_effects=True, vmem_limit_bytes=16 * 2**20
        ),
    )(blocks)


def general(queries, projection, lists, probes, owner_map):
    query_count, width = queries.shape
    probe_count = probes.shape[1]
    lists_here, list_size = lists.shape[0], lists.shape[1]
    device_count = lax.axis_size("grp") * lax.axis_size("own")
    pairs = query_count * probe_count
    capacity = 2 * pairs // device_count
    list_capacity = device_count * capacity // lists_here
    slots = device_count * capacity
    me = lax.axis_index(AXES)

    projected = jnp.dot(queries, projection, preferred_element_type=jnp.float32).astype(
        jnp.bfloat16
    )
    stored = jnp.take(owner_map, probes.reshape(-1))
    target = stored // lists_here
    local = stored % lists_here
    to_target = (target[:, None] == jnp.arange(device_count, dtype=jnp.int32)[None, :]).astype(
        jnp.bfloat16
    )
    step = jnp.arange(pairs, dtype=jnp.int32)
    earlier = (step[None, :] < step[:, None]).astype(jnp.bfloat16)
    before = jnp.dot(earlier, to_target, preferred_element_type=jnp.float32)
    rank = jnp.sum(before * to_target.astype(jnp.float32), axis=1).astype(jnp.int32)
    position = target * capacity + rank

    at_rank = (rank[:, None] == jnp.arange(capacity, dtype=jnp.int32)[None, :]).astype(jnp.bfloat16)
    query_of = step // probe_count
    what = jnp.stack([jnp.ones_like(step), query_of, local], axis=0).astype(jnp.bfloat16)
    weighted = to_target.T[None] * what[:, None, :]
    table = jnp.dot(
        weighted.reshape(3 * device_count, pairs), at_rank, preferred_element_type=jnp.float32
    ).reshape(3, device_count, capacity)
    table = jnp.where(table[:1] > 0.5, table[1:], -1.0).astype(jnp.bfloat16)
    columns = width // LANES
    extra = -(-(2 * slots) // (16 * LANES)) * 16
    table = jnp.pad(table.reshape(-1), (0, extra * LANES - 2 * slots)).reshape(extra, LANES)
    stacked = projected.reshape(query_count, columns, LANES).transpose(1, 0, 2)
    stacked = stacked.reshape(columns * query_count, LANES)

    everyone = lax.all_gather(jnp.concatenate([stacked, table], axis=0), AXES, tiled=False)
    tables = everyone[:, columns * query_count :].reshape(device_count, -1)[:, : 2 * slots]
    tables = tables.reshape(device_count, 2, device_count, capacity)
    mine = lax.dynamic_index_in_dim(tables, me, axis=2, keepdims=False).astype(jnp.int32)
    asked_query = mine[:, 0].reshape(-1)
    asked_list = mine[:, 1].reshape(-1)
    row_of = (
        asked_query + query_count * (jnp.arange(slots, dtype=jnp.int32) // capacity)
    )

    in_list = (asked_list[:, None] == jnp.arange(lists_here, dtype=jnp.int32)[None, :]).astype(
        jnp.bfloat16
    )
    place = jnp.arange(slots, dtype=jnp.int32)
    earlier = (place[None, :] < place[:, None]).astype(jnp.bfloat16)
    before = jnp.dot(earlier, in_list, preferred_element_type=jnp.float32)
    order = jnp.sum(before * in_list.astype(jnp.float32), axis=1).astype(jnp.int32)
    valid = asked_list >= 0
    spot = jnp.where(valid, asked_list * list_capacity + order, -1)
    hit = spot[:, None] == jnp.arange(lists_here * list_capacity, dtype=jnp.int32)[None, :]
    grouped_row = jnp.sum(jnp.where(hit, row_of[:, None], 0), axis=0)
    grouped = select_rows(everyone, grouped_row, query_count, width)
    blocks = score(grouped, lists, spot, device_count)
    answer_rows = capacity * list_size // LANES
    got = exchange(blocks).astype(jnp.float32)
    powers = got[:, answer_rows:].reshape(device_count, -1)[:, :capacity].reshape(slots, 1)
    returned = (
        got[:, :answer_rows]
        .reshape(device_count, list_size // LANES, capacity, LANES)
        .transpose(0, 2, 1, 3)
        .reshape(slots, list_size)
    )
    returned = (returned + 32768.0) * (jnp.exp2(powers) / 65535.0)
    return returned[position].reshape(query_count, probe_count, list_size)


PLANES = 4
PLANE = 8
TABLE = 16
BATCH = 8
CAPACITY = 32
VMEM_LIMIT = 56 * 2**20


def number(z, x, y, c):
    return z * PLANE + x * 4 + y * 2 + c


def mesh_id(n):
    return (n // 4, lax.rem(n, 4))


def ranks(mine):
    lane = lax.broadcasted_iota(jnp.int32, mine.shape, 1)
    within = mine
    for reach in (1, 2, 4, 8, 16, 32, 64):
        within = within + jnp.where(lane >= reach, pltpu.roll(within, reach, 1), 0.0)
    totals = jnp.broadcast_to(within[:, LANES - 1 :], mine.shape).reshape(-1, 8, LANES)
    probe = lax.broadcasted_iota(jnp.int32, totals.shape, 1)
    before = totals
    for reach in (1, 2, 4):
        before = before + jnp.where(probe >= reach, pltpu.roll(before, reach, 1), 0.0)
    return within - mine + (before - totals).reshape(mine.shape)


def fused_kernel(
    queries_hbm,
    projection_hbm,
    probes_hbm,
    owner_hbm,
    lists_hbm,
    out_hbm,
    queries_ref,
    projection_ref,
    probes_ref,
    owner_ref,
    all_ref,
    lists_ref,
    norms_ref,
    even_ref,
    odd_ref,
    send_ref,
    got_ref,
    place_ref,
    total_ref,
    out_ref,
    input_sem,
    list_sem,
    spread_send,
    spread_recv,
    back_send,
    back_recv,
    out_sem,
):
    grp, own = lax.axis_index("grp"), lax.axis_index("own")
    z, x, y, c = grp // 2, lax.rem(grp, 2), own // 2, lax.rem(own, 2)
    me = number(z, x, y, c)
    devices = all_ref.shape[0]
    query_count, width = queries_ref.shape
    list_count, list_size = lists_ref.shape[0], lists_ref.shape[1]
    columns = width // LANES
    table_at = columns * query_count
    capacity = CAPACITY

    inputs = [
        pltpu.make_async_copy(src, dst, input_sem.at[i])
        for i, (src, dst) in enumerate(
            (
                (projection_hbm, projection_ref),
                (queries_hbm, queries_ref),
                (probes_hbm, probes_ref),
                (owner_hbm, owner_ref),
            )
        )
    ]
    for copy in inputs:
        copy.start()
    barrier = pltpu.get_barrier_semaphore()

    near, cross, opposite = z + 1 - 2 * lax.rem(z, 2), lax.rem(z + 2, PLANES), PLANES - 1 - z
    xa, ya = x * c + (1 - x) * (1 - c), y * (1 - c) + (1 - y) * c
    xb, yb = x * (1 - c) + (1 - x) * c, y * c + (1 - y) * (1 - c)
    sides = {"o": (x, y), "a": (xa, ya), "b": (xb, yb), "d": (1 - x, 1 - y)}
    sides |= {"x": (1 - x, y), "y": (x, 1 - y)}

    def block_of(p, side, twin=False):
        return number(p, *sides[side], 1 - c if twin else c)

    peer_a, peer_b = block_of(z, "a"), block_of(z, "b")
    peer_near, peer_cross = block_of(near, "o"), block_of(cross, "o")
    sibling = block_of(z, "o", True)
    peers = (peer_cross, peer_a, peer_b, peer_near, sibling)
    for peer in peers:
        pl.semaphore_signal(
            barrier, inc=1, device_id=mesh_id(peer), device_id_type=pl.DeviceIdType.MESH
        )

    part = list_count // list_sem.shape[0]

    def list_copy(n):
        piece = pl.ds(n * part, part)
        return pltpu.make_async_copy(lists_hbm.at[piece], lists_ref.at[piece], list_sem.at[n])

    for copy in inputs:
        copy.wait()
    for n in range(list_sem.shape[0]):
        list_copy(n).start()

    projected = jnp.dot(
        queries_ref[...], projection_ref[...], preferred_element_type=jnp.float32
    ).astype(jnp.bfloat16)
    for j in range(columns):
        all_ref[me, j * query_count : (j + 1) * query_count, :] = projected[
            :, j * LANES : (j + 1) * LANES
        ]
    ids = jnp.concatenate([probes_ref[...], probes_ref[...]], axis=1)
    low, high = ids & (LANES - 1), ids >> 7
    stored = jnp.zeros_like(ids)
    for h in range(owner_ref.shape[0]):
        row = jnp.broadcast_to(owner_ref[h : h + 1, :], ids.shape)
        found = jnp.take_along_axis(row, low, axis=1, mode="promise_in_bounds")
        stored = jnp.where(high == h, found, stored)
    lane8 = lax.broadcasted_iota(jnp.int32, ids.shape, 1)
    table = jnp.where(lane8 < query_count, stored >> 5, stored & 31).astype(jnp.float32)
    all_ref[me, table_at:, :] = jnp.concatenate([table, jnp.zeros_like(table)], axis=0).astype(
        jnp.bfloat16
    )
    pl.semaphore_wait(barrier, len(peers))

    sent = []

    def describe(block, peer, slot):
        return pltpu.make_async_remote_copy(
            src_ref=all_ref.at[block],
            dst_ref=all_ref.at[block],
            send_sem=spread_send.at[slot],
            recv_sem=spread_recv.at[block],
            device_id=mesh_id(peer),
            device_id_type=pl.DeviceIdType.MESH,
        )

    def send(block, *peers):
        for peer in peers:
            copy = describe(block, peer, len(sent))
            copy.start()
            sent.append(copy)

    def arrived(block):
        describe(block, sibling, 0).wait_recv()

    def relay(p, side, *peers):
        arrived(block_of(p, side))
        send(block_of(p, side), *peers)

    send(me, *peers)

    def list_norms(first, last):
        for n in range(first, last):
            list_copy(n).wait()
            rows = []
            for i in range(n * part, (n + 1) * part):
                partial = None
                for j in range(columns):
                    piece = lists_ref[i, :, j * LANES : (j + 1) * LANES].astype(jnp.float32)
                    partial = piece * piece if partial is None else partial + piece * piece
                rows.append(0.5 * jnp.sum(partial.T, axis=0, keepdims=True))
            norms_ref[n * part : (n + 1) * part, :] = jnp.concatenate(rows, axis=0)

    list_norms(0, 5)
    relay(z, "a", sibling, peer_b)
    relay(z, "b", sibling)
    list_norms(5, 7)
    relay(cross, "o", peer_a, peer_b, sibling, peer_near)
    list_norms(7, 8)

    itself = (z, "o")
    batches = (
        (
            itself,
            (z, "o", True),
            (z, "x"),
            (z, "x", True),
            (z, "y"),
            (z, "y", True),
            (cross, "o"),
            (cross, "o", True),
        ),
        (
            (cross, "x"),
            (cross, "x", True),
            (cross, "y"),
            (cross, "y", True),
            (opposite, "o"),
            (opposite, "o", True),
            (near, "o"),
            (near, "o", True),
        ),
        (
            (cross, "d"),
            (cross, "d", True),
            (opposite, "x"),
            (opposite, "x", True),
            (opposite, "y"),
            (opposite, "y", True),
            (near, "x"),
            (near, "x", True),
        ),
        (
            (opposite, "d"),
            (opposite, "d", True),
            (z, "d"),
            (z, "d", True),
            (near, "y"),
            (near, "y", True),
            (near, "d"),
            (near, "d", True),
        ),
    )
    order = [block_of(*where).astype(jnp.float32) for chips in batches for where in chips]
    def back(n):
        return pltpu.make_async_remote_copy(
            src_ref=send_ref.at[n],
            dst_ref=got_ref.at[n],
            send_sem=back_send.at[n],
            recv_sem=back_recv.at[n],
            device_id=mesh_id(block_of(*batches[n // BATCH][n % BATCH])),
            device_id_type=pl.DeviceIdType.MESH,
        )

    me_f = me.astype(jnp.float32)
    slots = BATCH * capacity
    slot = lax.broadcasted_iota(jnp.int32, (capacity, LANES), 0).astype(jnp.float32)

    def choose(chips):
        tables = [
            all_ref[block_of(*where), table_at:, :].astype(jnp.float32)[:8, :] for where in chips
        ]
        tables = jnp.concatenate(tables, axis=0)
        lane = lax.broadcasted_iota(jnp.int32, tables.shape, 1)
        mine = jnp.where((lane < query_count) & (tables == me_f), 1.0, 0.0)
        rank = jnp.where(mine > 0.5, ranks(mine), -1.0)
        local = tables + 1.0
        at = (rank, pltpu.roll(rank, query_count, 1))
        what = (pltpu.roll(local, query_count, 1), local)
        picks, lists_of = [], []
        for t in range(BATCH):
            pick = jnp.zeros((capacity, LANES), jnp.float32)
            which = jnp.zeros((capacity, LANES), jnp.float32)
            for j in range(8):
                row = t * 8 + j
                hit = at[t % 2][row : row + 1, :] == slot
                pick = jnp.where(hit, 1.0, pick)
                which = jnp.where(hit, what[t % 2][row : row + 1, :], which)
            picks.append(pick.astype(jnp.bfloat16))
            lists_of.append(which)
        place = jnp.sum(jnp.concatenate(lists_of, axis=0), axis=1, keepdims=True)
        place = jnp.broadcast_to(place, (slots, LANES))
        return picks, place

    def select(chips, picks, picked):
        norm = jnp.zeros((slots, LANES), jnp.float32)
        for j in range(columns):
            rows = []
            for u in range(0, BATCH, 2):
                pair = [
                    all_ref[block_of(*where), j * query_count : (j + 1) * query_count, :]
                    for where in chips[u : u + 2]
                ]
                pair = jnp.concatenate(pair, axis=0)
                pick = jnp.concatenate(picks[u : u + 2], axis=0)
                rows.append(jnp.dot(pick, pair, preferred_element_type=jnp.float32))
            piece = jnp.concatenate(rows, axis=0)
            norm = norm + piece * piece
            picked[:, j * LANES : (j + 1) * LANES] = piece.astype(jnp.bfloat16)
        return jnp.sum(norm, axis=1, keepdims=True)

    def encode(k, best, norm):
        distance = jnp.maximum((norm - 2.0 * best) * (1.0 / width), 0.0)
        largest = jnp.maximum(jnp.max(distance, axis=1, keepdims=True), 1e-30)
        power = jnp.clip(jnp.ceil(jnp.log(largest) * LOG2E + 1e-3), -100.0, 120.0)
        code = jnp.clip(jnp.round(distance * (65535.0 * jnp.exp(power * -LN2))), 0.0, 65535.0)
        code = code.astype(jnp.int32)
        word = code[:, :LANES] | (code[:, LANES:] << 16)
        whole = (BATCH, capacity, LANES)
        word = word.reshape(whole)
        quarter = lax.broadcasted_iota(jnp.int32, whole, 0) & 3
        spot = lax.broadcasted_iota(jnp.int32, whole, 1) + quarter * capacity
        lane = lax.broadcasted_iota(jnp.int32, whole, 2)
        powers = jnp.broadcast_to(power, (slots, LANES)).reshape(whole)
        powers = jnp.sum(jnp.where(spot == lane, powers, 0.0), axis=1, keepdims=True)
        powers = powers.astype(jnp.int32)
        send_ref[k * BATCH : (k + 1) * BATCH, :capacity, :] = word
        send_ref[k * BATCH : (k + 1) * BATCH, capacity : capacity + 1, :] = powers

    returned = []

    def others(k):
        return [back(n) for n in range(max(k * BATCH, 1), (k + 1) * BATCH)]

    def give_back(k):
        for copy in others(k):
            copy.start()
            returned.append(copy)

    relays = {
        (0, 2): ((opposite, "o", peer_a, peer_b, sibling),),
        (0, 3): (
            (cross, "a", peer_b, sibling),
            (cross, "b", sibling),
            (z, "d", peer_near, sibling),
        ),
        (1, 2): (
            (cross, "d", peer_near, sibling),
            (opposite, "a", sibling),
            (opposite, "b", sibling),
            (near, "a", sibling),
            (near, "b", sibling),
        ),
        (2, 1): ((near, "d", sibling), (opposite, "d", sibling)),
    }
    picked_refs = (even_ref, odd_ref)

    def prepare(k):
        for where in batches[k]:
            if len(where) == 3:
                arrived(block_of(*where))
        return choose(batches[k])

    def score(k, place, best, first, count):
        dots = lax.dot_general(
            picked_refs[k % 2][...],
            lists_ref[first : first + count].reshape(count * list_size, width),
            (((1,), (1,)), ((), ())),
            preferred_element_type=jnp.float32,
        )
        for i in range(count):
            n = first + i
            hit = place == n + 1.0
            hit = jnp.concatenate([hit] * (list_size // LANES), axis=1)
            value = dots[:, i * list_size : (i + 1) * list_size] - norms_ref[n : n + 1, :]
            best = jnp.where(hit, value, best)
        return best

    step = list_count // 4
    for where in batches[0]:
        if len(where) == 3:
            arrived(block_of(*where))
    relay(near, "o", peer_a, peer_b, sibling)
    picks, place = choose(batches[0])
    norm = select(batches[0], picks, picked_refs[0])
    for k, chips in enumerate(batches):
        best = jnp.zeros((slots, list_size), jnp.float32)
        begin = 0
        for stop in (1, 2, 3):
            relayed = relays.get((k, stop), ())
            if relayed or (stop == 3 and 0 < k < 3):
                best = score(k, place, best, begin * step, (stop - begin) * step)
                begin = stop
                for item in relayed:
                    relay(*item)
        ahead = 0 < k < len(batches) - 1
        if ahead:
            picks, later = prepare(k + 1)
        best = score(k, place, best, begin * step, (4 - begin) * step)
        if ahead:
            after = select(batches[k + 1], picks, picked_refs[(k + 1) % 2])
        encode(k, best, norm)
        give_back(k)
        if k == 0:
            picks, later = prepare(1)
            after = select(batches[1], picks, picked_refs[1])
        place, norm = later, after
    got_ref[0] = send_ref[0]

    target = jnp.where(lane8 < query_count, (stored >> 5).astype(jnp.float32), -1.0)
    mine = jnp.concatenate([jnp.where(target == d, 1.0, 0.0) for d in order], axis=0)
    rank = ranks(mine)
    spot = jnp.zeros(ids.shape, jnp.float32)
    for n, d in enumerate(order):
        spot = jnp.where(target == d, rank[n * 8 : (n + 1) * 8] + float(n * capacity), spot)
    wide = lax.broadcasted_iota(jnp.int32, (8, devices * capacity), 1).astype(jnp.float32)
    for q in range(0, query_count, 2):
        both = [jnp.where(spot[:, i : i + 1] == wide, 1.0, 0.0) for i in (q, q + 1)]
        place_ref[q * 8 : (q + 2) * 8, :] = jnp.concatenate(both, axis=0).astype(jnp.bfloat16)


    def receive(k):
        for copy in others(k):
            copy.wait_recv()

    def unpack(k, count):
        mine = slice(k * BATCH, (k + count) * BATCH)
        words = got_ref[mine, :capacity, :].reshape(count * slots, LANES)
        codes = [((words >> s) & 255).astype(jnp.float32) for s in (0, 8, 16, 24)]
        codes = jnp.concatenate([p.astype(jnp.bfloat16) for p in codes], axis=1)
        powers = got_ref[mine, capacity : capacity + 1, :].astype(jnp.float32)
        powers = jnp.sum(powers.reshape(count * BATCH // 4, 4, LANES), axis=1)
        powers = jnp.concatenate(
            [jnp.broadcast_to(powers[g : g + 1], (LANES, LANES)) for g in range(powers.shape[0])],
            axis=1,
        ).astype(jnp.bfloat16)
        return codes, powers

    def gather(codes, powers, rows, k):
        place = place_ref[rows, k * slots : k * slots + codes.shape[0]]
        chosen = jnp.dot(place, codes, preferred_element_type=jnp.float32)
        power = lax.dot_general(
            place, powers, (((1,), (1,)), ((), ())), preferred_element_type=jnp.float32
        )
        return jnp.concatenate([chosen, power], axis=1)

    for k in range(len(batches) - 1):
        receive(k)
    final = len(batches) - 1
    total_ref[...] = gather(*unpack(0, final), slice(None), 0)
    receive(final)
    unpacked = unpack(final, 1)
    results = []
    half = out_ref.shape[0] // 2
    for n in range(2):
        rows = slice(n * half, (n + 1) * half)
        total = total_ref[rows, :] + gather(*unpacked, rows, final)
        scale = jnp.exp(total[:, 4 * LANES :] * LN2) * (1.0 / 65535.0)
        for h in range(2):
            low = total[:, 2 * h * LANES : (2 * h + 1) * LANES]
            high = total[:, (2 * h + 1) * LANES : (2 * h + 2) * LANES]
            out_ref[rows, h * LANES : (h + 1) * LANES] = (low + 256.0 * high) * scale
        part_of = pl.ds(n * half, half)
        results.append(pltpu.make_async_copy(out_ref.at[part_of], out_hbm.at[part_of], out_sem.at[n]))
        results[-1].start()
    for copy in sent:
        copy.wait_send()
    for copy in returned:
        copy.wait_send()
    for copy in results:
        copy.wait()


def fused(queries, projection, lists, probes, owner_map):
    query_count, width = queries.shape
    probe_count = probes.shape[1]
    list_count, list_size = lists.shape[0], lists.shape[1]
    devices = PLANES * PLANE
    pairs, slots = query_count * probe_count, devices * CAPACITY
    rows = width // LANES * query_count + TABLE
    hbm = pl.BlockSpec(memory_space=pltpu.HBM)
    owners = owner_map.reshape(-1, LANES)
    words = (devices, CAPACITY + 1, LANES)
    scores = pl.pallas_call(
        fused_kernel,
        out_shape=jax.ShapeDtypeStruct((pairs, list_size), jnp.float32),
        in_specs=[hbm] * 5,
        out_specs=hbm,
        scratch_shapes=[
            pltpu.VMEM(queries.shape, jnp.bfloat16),
            pltpu.VMEM(projection.shape, jnp.bfloat16),
            pltpu.VMEM((probe_count, query_count), jnp.int32),
            pltpu.VMEM(owners.shape, jnp.int32),
            pltpu.VMEM((devices, rows, LANES), jnp.bfloat16),
            pltpu.VMEM(lists.shape, jnp.bfloat16),
            pltpu.VMEM((list_count, list_size), jnp.float32),
            pltpu.VMEM((BATCH * CAPACITY, width), jnp.bfloat16),
            pltpu.VMEM((BATCH * CAPACITY, width), jnp.bfloat16),
            pltpu.VMEM(words, jnp.int32),
            pltpu.VMEM(words, jnp.int32),
            pltpu.VMEM((pairs, slots), jnp.bfloat16),
            pltpu.VMEM((pairs, 5 * LANES), jnp.float32),
            pltpu.VMEM((pairs, list_size), jnp.float32),
            pltpu.SemaphoreType.DMA((4,)),
            pltpu.SemaphoreType.DMA((8,)),
            pltpu.SemaphoreType.DMA((devices,)),
            pltpu.SemaphoreType.DMA((devices,)),
            pltpu.SemaphoreType.DMA((devices,)),
            pltpu.SemaphoreType.DMA((devices,)),
            pltpu.SemaphoreType.DMA((2,)),
        ],
        compiler_params=pltpu.CompilerParams(
            collective_id=0, has_side_effects=True, vmem_limit_bytes=VMEM_LIMIT
        ),
    )(queries, projection, probes.T, owners, lists)
    return scores.reshape(query_count, probe_count, list_size)


def solution(mesh):
    placed = (
        P(AXES, None),
        P(),
        P(AXES, None, None),
        P(AXES, None),
        P(),
    )
    sizes = (mesh.shape["grp"], mesh.shape["own"])
    return jax.shard_map(
        fused if sizes == (8, 4) else general,
        mesh=mesh,
        in_specs=placed,
        out_specs=P(AXES, None, None),
        check_vma=False,
    )
```

```python
import jax
import jax.numpy as jnp
from jax import lax
from jax.experimental import pallas as pl
from jax.experimental.pallas import tpu as pltpu
from jax.sharding import PartitionSpec as P

AXES = ("grp", "own")
LANES = 128
LOG2E = 1.4426950408889634
LN2 = 0.6931471805599453


def select_kernel(queries, width, row_ref, all_ref, out_ref):
    devices = all_ref.shape[0]
    count = out_ref.shape[0]
    numbers = lax.broadcasted_iota(jnp.int32, (count, devices * queries), 1)
    pick = (numbers == row_ref[...]).astype(jnp.float32).astype(jnp.bfloat16)
    for j in range(width // LANES):
        part = all_ref[:, j * queries : (j + 1) * queries, :].reshape(devices * queries, LANES)
        out_ref[:, j * LANES : (j + 1) * LANES] = jnp.dot(
            pick, part, preferred_element_type=jnp.float32
        ).astype(jnp.bfloat16)


def select_rows(everyone, row_of, queries, width):
    slots = row_of.shape[0]
    block = min(256, slots)
    return pl.pallas_call(
        lambda *refs: select_kernel(queries, width, *refs),
        grid=(slots // block,),
        out_shape=jax.ShapeDtypeStruct((slots, width), jnp.bfloat16),
        in_specs=[
            pl.BlockSpec((block, 1), lambda i: (i, 0)),
            pl.BlockSpec(memory_space=pltpu.VMEM),
        ],
        out_specs=pl.BlockSpec((block, width), lambda i: (i, 0)),
        compiler_params=pltpu.CompilerParams(vmem_limit_bytes=48 * 2**20),
    )(row_of[:, None], everyone)


def score_kernel(blocks, rows_ref, lists_ref, spot_ref, out_ref, held):
    step = pl.program_id(0)
    count, list_size, width = lists_ref.shape
    capacity = rows_ref.shape[0] // count
    for n in range(count):
        rows = rows_ref[n * capacity : (n + 1) * capacity, :]
        dots = lax.dot_general(
            rows, lists_ref[n], (((1,), (1,)), ((), ())), preferred_element_type=jnp.float32
        )
        rows_f = rows.astype(jnp.float32)
        row_norm = jnp.sum(rows_f * rows_f, axis=1, keepdims=True)
        partial = None
        for j in range(width // LANES):
            part = lists_ref[n, :, j * LANES : (j + 1) * LANES].astype(jnp.float32)
            partial = part * part if partial is None else partial + part * part
        vec_norm = jnp.sum(partial.T, axis=0, keepdims=True)
        distance = jnp.maximum((row_norm + vec_norm - 2.0 * dots) / width, 0.0)
        largest = jnp.maximum(jnp.max(distance, axis=1, keepdims=True), 1e-30)
        power = jnp.clip(jnp.ceil(jnp.log(largest) * LOG2E + 1e-3), -100.0, 120.0)
        code = jnp.clip(jnp.round(distance * (65535.0 * jnp.exp(power * -LN2))), 0.0, 65535.0)
        high = jnp.floor(code * (1.0 / 256.0))
        low = code - high * 256.0
        place = pl.ds(pl.multiple_of((step * count + n) * capacity, 16), capacity)
        held[place, :list_size] = high.astype(jnp.bfloat16)
        held[place, list_size : 2 * list_size] = low.astype(jnp.bfloat16)
        held[place, 2 * list_size :] = jnp.broadcast_to(power, (capacity, LANES)).astype(
            jnp.bfloat16
        )

    @pl.when(step == pl.num_programs(0) - 1)
    def _():
        slots = held.shape[0]
        each = slots // blocks
        numbers = lax.broadcasted_iota(jnp.int32, (slots, slots), 1)
        pick = (numbers == spot_ref[...]).astype(jnp.float32).astype(jnp.bfloat16)
        got = jnp.dot(pick, held[...], preferred_element_type=jnp.float32)
        code = got[:, :list_size] * 256.0 + got[:, list_size : 2 * list_size] - 32768.0
        parts = [
            code[:, h * LANES : (h + 1) * LANES].reshape(blocks, each, LANES)
            for h in range(list_size // LANES)
        ]
        powers = got[:, 2 * list_size :].reshape(blocks, each, LANES)
        slot = lax.broadcasted_iota(jnp.int32, powers.shape, 1)
        lane = lax.broadcasted_iota(jnp.int32, powers.shape, 2)
        powers = jnp.sum(jnp.where(slot == lane, powers, 0.0), axis=1, keepdims=True)
        parts.append(jnp.broadcast_to(powers, (blocks, 16, LANES)))
        whole = jnp.concatenate(parts, axis=1)
        out_ref[...] = whole.astype(jnp.int32).astype(jnp.int16)


def score(grouped, lists, spot, blocks):
    list_count, list_size, width = lists.shape
    slots = grouped.shape[0]
    count = 4
    out_rows = (slots // blocks) * list_size // LANES + 16
    return pl.pallas_call(
        lambda *refs: score_kernel(blocks, *refs),
        grid=(list_count // count,),
        out_shape=jax.ShapeDtypeStruct((blocks, out_rows, LANES), jnp.int16),
        in_specs=[
            pl.BlockSpec((slots // list_count * count, width), lambda i: (i, 0)),
            pl.BlockSpec((count, list_size, width), lambda i: (i, 0, 0)),
            pl.BlockSpec((slots, 1), lambda i: (0, 0)),
        ],
        out_specs=pl.BlockSpec((blocks, out_rows, LANES), lambda i: (0, 0, 0)),
        scratch_shapes=[pltpu.VMEM((slots, 2 * list_size + LANES), jnp.bfloat16)],
        compiler_params=pltpu.CompilerParams(vmem_limit_bytes=40 * 2**20),
    )(grouped, lists, spot[:, None])


def exchange_kernel(device_count, owner_count, out_ref, in_ref, send_sem, recv_sem):
    me = lax.axis_index("grp") * owner_count + lax.axis_index("own")

    def at(k):
        other = lax.rem(me + k, device_count)
        return other, (other // owner_count, lax.rem(other, owner_count))

    barrier = pltpu.get_barrier_semaphore()

    @pl.loop(1, device_count)
    def _(k):
        pl.semaphore_signal(
            barrier, inc=1, device_id=at(k)[1], device_id_type=pl.DeviceIdType.MESH
        )

    pl.semaphore_wait(barrier, device_count - 1)

    def describe(k, block):
        other, where = at(k)
        return pltpu.make_async_remote_copy(
            src_ref=out_ref.at[other],
            dst_ref=in_ref.at[block],
            send_sem=send_sem.at[k],
            recv_sem=recv_sem.at[block],
            device_id=where,
            device_id_type=pl.DeviceIdType.MESH,
        )

    @pl.loop(1, device_count)
    def _(k):
        describe(k, me).start()

    in_ref[me] = out_ref[me]

    @pl.loop(1, device_count)
    def _(k):
        describe(k, at(k)[0]).wait_recv()

    @pl.loop(1, device_count)
    def _(k):
        describe(k, me).wait_send()


def exchange(blocks):
    owner_count = lax.axis_size("own")
    device_count = blocks.shape[0]
    return pl.pallas_call(
        lambda *refs: exchange_kernel(device_count, owner_count, *refs),
        out_shape=jax.ShapeDtypeStruct(blocks.shape, blocks.dtype),
        in_specs=[pl.BlockSpec(memory_space=pltpu.VMEM)],
        out_specs=pl.BlockSpec(memory_space=pltpu.VMEM),
        scratch_shapes=[
            pltpu.SemaphoreType.DMA((device_count,)),
            pltpu.SemaphoreType.DMA((device_count,)),
        ],
        compiler_params=pltpu.CompilerParams(
            collective_id=1, has_side_effects=True, vmem_limit_bytes=16 * 2**20
        ),
    )(blocks)


def general(queries, projection, lists, probes, owner_map):
    query_count, width = queries.shape
    probe_count = probes.shape[1]
    lists_here, list_size = lists.shape[0], lists.shape[1]
    device_count = lax.axis_size("grp") * lax.axis_size("own")
    pairs = query_count * probe_count
    capacity = 2 * pairs // device_count
    list_capacity = device_count * capacity // lists_here
    slots = device_count * capacity
    me = lax.axis_index(AXES)

    projected = jnp.dot(queries, projection, preferred_element_type=jnp.float32).astype(
        jnp.bfloat16
    )
    stored = jnp.take(owner_map, probes.reshape(-1))
    target = stored // lists_here
    local = stored % lists_here
    to_target = (target[:, None] == jnp.arange(device_count, dtype=jnp.int32)[None, :]).astype(
        jnp.bfloat16
    )
    step = jnp.arange(pairs, dtype=jnp.int32)
    earlier = (step[None, :] < step[:, None]).astype(jnp.bfloat16)
    before = jnp.dot(earlier, to_target, preferred_element_type=jnp.float32)
    rank = jnp.sum(before * to_target.astype(jnp.float32), axis=1).astype(jnp.int32)
    position = target * capacity + rank

    at_rank = (rank[:, None] == jnp.arange(capacity, dtype=jnp.int32)[None, :]).astype(jnp.bfloat16)
    query_of = step // probe_count
    what = jnp.stack([jnp.ones_like(step), query_of, local], axis=0).astype(jnp.bfloat16)
    weighted = to_target.T[None] * what[:, None, :]
    table = jnp.dot(
        weighted.reshape(3 * device_count, pairs), at_rank, preferred_element_type=jnp.float32
    ).reshape(3, device_count, capacity)
    table = jnp.where(table[:1] > 0.5, table[1:], -1.0).astype(jnp.bfloat16)
    columns = width // LANES
    extra = -(-(2 * slots) // (16 * LANES)) * 16
    table = jnp.pad(table.reshape(-1), (0, extra * LANES - 2 * slots)).reshape(extra, LANES)
    stacked = projected.reshape(query_count, columns, LANES).transpose(1, 0, 2)
    stacked = stacked.reshape(columns * query_count, LANES)

    everyone = lax.all_gather(jnp.concatenate([stacked, table], axis=0), AXES, tiled=False)
    tables = everyone[:, columns * query_count :].reshape(device_count, -1)[:, : 2 * slots]
    tables = tables.reshape(device_count, 2, device_count, capacity)
    mine = lax.dynamic_index_in_dim(tables, me, axis=2, keepdims=False).astype(jnp.int32)
    asked_query = mine[:, 0].reshape(-1)
    asked_list = mine[:, 1].reshape(-1)
    row_of = (
        asked_query + query_count * (jnp.arange(slots, dtype=jnp.int32) // capacity)
    )

    in_list = (asked_list[:, None] == jnp.arange(lists_here, dtype=jnp.int32)[None, :]).astype(
        jnp.bfloat16
    )
    place = jnp.arange(slots, dtype=jnp.int32)
    earlier = (place[None, :] < place[:, None]).astype(jnp.bfloat16)
    before = jnp.dot(earlier, in_list, preferred_element_type=jnp.float32)
    order = jnp.sum(before * in_list.astype(jnp.float32), axis=1).astype(jnp.int32)
    valid = asked_list >= 0
    spot = jnp.where(valid, asked_list * list_capacity + order, -1)
    hit = spot[:, None] == jnp.arange(lists_here * list_capacity, dtype=jnp.int32)[None, :]
    grouped_row = jnp.sum(jnp.where(hit, row_of[:, None], 0), axis=0)
    grouped = select_rows(everyone, grouped_row, query_count, width)
    blocks = score(grouped, lists, spot, device_count)
    answer_rows = capacity * list_size // LANES
    got = exchange(blocks).astype(jnp.float32)
    powers = got[:, answer_rows:].reshape(device_count, -1)[:, :capacity].reshape(slots, 1)
    returned = (
        got[:, :answer_rows]
        .reshape(device_count, list_size // LANES, capacity, LANES)
        .transpose(0, 2, 1, 3)
        .reshape(slots, list_size)
    )
    returned = (returned + 32768.0) * (jnp.exp2(powers) / 65535.0)
    return returned[position].reshape(query_count, probe_count, list_size)


PLANES = 4
PLANE = 8
TABLE = 16
BATCH = 8
CAPACITY = 32
VMEM_LIMIT = 56 * 2**20


def number(z, x, y, c):
    return z * PLANE + x * 4 + y * 2 + c


def mesh_id(n):
    return (n // 4, lax.rem(n, 4))


def ranks(mine):
    lane = lax.broadcasted_iota(jnp.int32, mine.shape, 1)
    within = mine
    for reach in (1, 2, 4, 8, 16, 32, 64):
        within = within + jnp.where(lane >= reach, pltpu.roll(within, reach, 1), 0.0)
    totals = jnp.broadcast_to(within[:, LANES - 1 :], mine.shape).reshape(-1, 8, LANES)
    probe = lax.broadcasted_iota(jnp.int32, totals.shape, 1)
    before = totals
    for reach in (1, 2, 4):
        before = before + jnp.where(probe >= reach, pltpu.roll(before, reach, 1), 0.0)
    return within - mine + (before - totals).reshape(mine.shape)


def fused_kernel(
    queries_hbm,
    projection_hbm,
    probes_hbm,
    owner_hbm,
    lists_hbm,
    out_hbm,
    queries_ref,
    projection_ref,
    probes_ref,
    owner_ref,
    all_ref,
    lists_ref,
    norms_ref,
    even_ref,
    odd_ref,
    send_ref,
    got_ref,
    place_ref,
    total_ref,
    out_ref,
    input_sem,
    list_sem,
    spread_send,
    spread_recv,
    back_send,
    back_recv,
    out_sem,
):
    grp, own = lax.axis_index("grp"), lax.axis_index("own")
    z, x, y, c = grp // 2, lax.rem(grp, 2), own // 2, lax.rem(own, 2)
    me = number(z, x, y, c)
    devices = all_ref.shape[0]
    query_count, width = queries_ref.shape
    list_count, list_size = lists_ref.shape[0], lists_ref.shape[1]
    columns = width // LANES
    table_at = columns * query_count
    capacity = CAPACITY

    inputs = [
        pltpu.make_async_copy(src, dst, input_sem.at[i])
        for i, (src, dst) in enumerate(
            (
                (projection_hbm, projection_ref),
                (queries_hbm, queries_ref),
                (probes_hbm, probes_ref),
                (owner_hbm, owner_ref),
            )
        )
    ]
    for copy in inputs:
        copy.start()
    barrier = pltpu.get_barrier_semaphore()

    near, cross, opposite = z + 1 - 2 * lax.rem(z, 2), lax.rem(z + 2, PLANES), PLANES - 1 - z
    xa, ya = x * c + (1 - x) * (1 - c), y * (1 - c) + (1 - y) * c
    xb, yb = x * (1 - c) + (1 - x) * c, y * c + (1 - y) * (1 - c)
    sides = {"o": (x, y), "a": (xa, ya), "b": (xb, yb), "d": (1 - x, 1 - y)}
    sides |= {"x": (1 - x, y), "y": (x, 1 - y)}

    def block_of(p, side, twin=False):
        return number(p, *sides[side], 1 - c if twin else c)

    peer_a, peer_b = block_of(z, "a"), block_of(z, "b")
    peer_near, peer_cross = block_of(near, "o"), block_of(cross, "o")
    sibling = block_of(z, "o", True)
    peers = (peer_cross, peer_a, peer_b, peer_near, sibling)
    for peer in peers:
        pl.semaphore_signal(
            barrier, inc=1, device_id=mesh_id(peer), device_id_type=pl.DeviceIdType.MESH
        )

    part = list_count // list_sem.shape[0]

    def list_copy(n):
        piece = pl.ds(n * part, part)
        return pltpu.make_async_copy(lists_hbm.at[piece], lists_ref.at[piece], list_sem.at[n])

    for copy in inputs:
        copy.wait()
    for n in range(list_sem.shape[0]):
        list_copy(n).start()

    projected = jnp.dot(
        queries_ref[...], projection_ref[...], preferred_element_type=jnp.float32
    ).astype(jnp.bfloat16)
    for j in range(columns):
        all_ref[me, j * query_count : (j + 1) * query_count, :] = projected[
            :, j * LANES : (j + 1) * LANES
        ]
    ids = jnp.concatenate([probes_ref[...], probes_ref[...]], axis=1)
    low, high = ids & (LANES - 1), ids >> 7
    stored = jnp.zeros_like(ids)
    for h in range(owner_ref.shape[0]):
        row = jnp.broadcast_to(owner_ref[h : h + 1, :], ids.shape)
        found = jnp.take_along_axis(row, low, axis=1, mode="promise_in_bounds")
        stored = jnp.where(high == h, found, stored)
    lane8 = lax.broadcasted_iota(jnp.int32, ids.shape, 1)
    table = jnp.where(lane8 < query_count, stored >> 5, stored & 31).astype(jnp.float32)
    all_ref[me, table_at:, :] = jnp.concatenate([table, jnp.zeros_like(table)], axis=0).astype(
        jnp.bfloat16
    )
    pl.semaphore_wait(barrier, len(peers))

    sent = []

    def describe(block, peer, slot):
        return pltpu.make_async_remote_copy(
            src_ref=all_ref.at[block],
            dst_ref=all_ref.at[block],
            send_sem=spread_send.at[slot],
            recv_sem=spread_recv.at[block],
            device_id=mesh_id(peer),
            device_id_type=pl.DeviceIdType.MESH,
        )

    def send(block, *peers):
        for peer in peers:
            copy = describe(block, peer, len(sent))
            copy.start()
            sent.append(copy)

    def arrived(block):
        describe(block, sibling, 0).wait_recv()

    def relay(p, side, *peers):
        arrived(block_of(p, side))
        send(block_of(p, side), *peers)

    send(me, *peers)

    def list_norms(first, last):
        for n in range(first, last):
            list_copy(n).wait()
            rows = []
            for i in range(n * part, (n + 1) * part):
                partial = None
                for j in range(columns):
                    piece = lists_ref[i, :, j * LANES : (j + 1) * LANES].astype(jnp.float32)
                    partial = piece * piece if partial is None else partial + piece * piece
                rows.append(0.5 * jnp.sum(partial.T, axis=0, keepdims=True))
            norms_ref[n * part : (n + 1) * part, :] = jnp.concatenate(rows, axis=0)

    list_norms(0, 5)
    relay(z, "a", sibling, peer_b)
    relay(z, "b", sibling)
    list_norms(5, 7)
    relay(cross, "o", peer_a, peer_b, sibling, peer_near)
    list_norms(7, 8)

    itself = (z, "o")
    batches = (
        (
            itself,
            (z, "x"),
            (z, "y"),
            (cross, "o"),
            (z, "o", True),
            (z, "x", True),
            (z, "y", True),
            (cross, "o", True),
        ),
        (
            (cross, "x"),
            (cross, "y"),
            (opposite, "o"),
            (near, "o"),
            (cross, "x", True),
            (cross, "y", True),
            (opposite, "o", True),
            (near, "o", True),
        ),
        (
            (cross, "d"),
            (cross, "d", True),
            (opposite, "x"),
            (opposite, "x", True),
            (opposite, "y"),
            (opposite, "y", True),
            (near, "x"),
            (near, "x", True),
        ),
        (
            (opposite, "d"),
            (opposite, "d", True),
            (z, "d"),
            (z, "d", True),
            (near, "y"),
            (near, "y", True),
            (near, "d"),
            (near, "d", True),
        ),
    )
    order = [block_of(*where).astype(jnp.float32) for chips in batches for where in chips]
    def back(n):
        return pltpu.make_async_remote_copy(
            src_ref=send_ref.at[n],
            dst_ref=got_ref.at[n],
            send_sem=back_send.at[n],
            recv_sem=back_recv.at[n],
            device_id=mesh_id(block_of(*batches[n // BATCH][n % BATCH])),
            device_id_type=pl.DeviceIdType.MESH,
        )

    me_f = me.astype(jnp.float32)
    slots = BATCH * capacity
    slot = lax.broadcasted_iota(jnp.int32, (capacity, LANES), 0).astype(jnp.float32)

    def choose(chips):
        tables = [
            all_ref[block_of(*where), table_at:, :].astype(jnp.float32)[:8, :] for where in chips
        ]
        tables = jnp.concatenate(tables, axis=0)
        lane = lax.broadcasted_iota(jnp.int32, tables.shape, 1)
        mine = jnp.where((lane < query_count) & (tables == me_f), 1.0, 0.0)
        rank = jnp.where(mine > 0.5, ranks(mine), -1.0)
        local = tables + 1.0
        at = (rank, pltpu.roll(rank, query_count, 1))
        what = (pltpu.roll(local, query_count, 1), local)
        picks, lists_of = [], []
        for t in range(len(chips)):
            pick = jnp.zeros((capacity, LANES), jnp.float32)
            which = jnp.zeros((capacity, LANES), jnp.float32)
            for j in range(8):
                row = t * 8 + j
                hit = at[t % 2][row : row + 1, :] == slot
                pick = jnp.where(hit, 1.0, pick)
                which = jnp.where(hit, what[t % 2][row : row + 1, :], which)
            picks.append(pick.astype(jnp.bfloat16))
            lists_of.append(which)
        place = jnp.sum(jnp.concatenate(lists_of, axis=0), axis=1, keepdims=True)
        place = jnp.broadcast_to(place, (place.shape[0], LANES))
        return picks, place

    def join(one, two):
        return one[0] + two[0], jnp.concatenate([one[1], two[1]], axis=0)

    def select(chips, picks, picked):
        norm = jnp.zeros((slots, LANES), jnp.float32)
        for j in range(columns):
            rows = []
            for u in range(0, BATCH, 2):
                pair = [
                    all_ref[block_of(*where), j * query_count : (j + 1) * query_count, :]
                    for where in chips[u : u + 2]
                ]
                pair = jnp.concatenate(pair, axis=0)
                pick = jnp.concatenate(picks[u : u + 2], axis=0)
                rows.append(jnp.dot(pick, pair, preferred_element_type=jnp.float32))
            piece = jnp.concatenate(rows, axis=0)
            norm = norm + piece * piece
            picked[:, j * LANES : (j + 1) * LANES] = piece.astype(jnp.bfloat16)
        return jnp.sum(norm, axis=1, keepdims=True)

    def encode(k, best, norm):
        distance = jnp.maximum((norm - 2.0 * best) * (1.0 / width), 0.0)
        largest = jnp.maximum(jnp.max(distance, axis=1, keepdims=True), 1e-30)
        power = jnp.clip(jnp.ceil(jnp.log(largest) * LOG2E + 1e-3), -100.0, 120.0)
        code = jnp.clip(jnp.round(distance * (65535.0 * jnp.exp(power * -LN2))), 0.0, 65535.0)
        code = code.astype(jnp.int32)
        word = code[:, :LANES] | (code[:, LANES:] << 16)
        whole = (BATCH, capacity, LANES)
        word = word.reshape(whole)
        quarter = lax.broadcasted_iota(jnp.int32, whole, 0) & 3
        spot = lax.broadcasted_iota(jnp.int32, whole, 1) + quarter * capacity
        lane = lax.broadcasted_iota(jnp.int32, whole, 2)
        powers = jnp.broadcast_to(power, (slots, LANES)).reshape(whole)
        powers = jnp.sum(jnp.where(spot == lane, powers, 0.0), axis=1, keepdims=True)
        powers = powers.astype(jnp.int32)
        send_ref[k * BATCH : (k + 1) * BATCH, :capacity, :] = word
        send_ref[k * BATCH : (k + 1) * BATCH, capacity : capacity + 1, :] = powers

    returned = []

    def others(k):
        return [back(n) for n in range(max(k * BATCH, 1), (k + 1) * BATCH)]

    def give_back(copies):
        for copy in copies:
            copy.start()
            returned.append(copy)

    relays = {
        (0, 2): ((opposite, "o", peer_a, peer_b, sibling),),
        (0, 3): (
            (cross, "a", peer_b, sibling),
            (cross, "b", sibling),
            (z, "d", peer_near, sibling),
        ),
        (1, 2): (
            (cross, "d", peer_near, sibling),
            (opposite, "a", sibling),
            (opposite, "b", sibling),
            (near, "a", sibling),
            (near, "b", sibling),
        ),
        (2, 1): (
            (near, "d", sibling),
            (opposite, "d", sibling),
        ),
    }
    picked_refs = (even_ref, odd_ref)

    def complete(k):
        for where in batches[k]:
            if len(where) == 3:
                arrived(block_of(*where))

    def score(k, place, best, first, count):
        dots = lax.dot_general(
            picked_refs[k % 2][...],
            lists_ref[first : first + count].reshape(count * list_size, width),
            (((1,), (1,)), ((), ())),
            preferred_element_type=jnp.float32,
        )
        for i in range(count):
            n = first + i
            hit = place == n + 1.0
            hit = jnp.concatenate([hit] * (list_size // LANES), axis=1)
            value = dots[:, i * list_size : (i + 1) * list_size] - norms_ref[n : n + 1, :]
            best = jnp.where(hit, value, best)
        return best

    step = list_count // 4
    direct = BATCH // 2
    early = choose(batches[0][:direct])
    complete(0)
    relay(near, "o", sibling, peer_a, peer_b)
    picks, place = join(early, choose(batches[0][direct:]))
    norm = select(batches[0], picks, picked_refs[0])
    for k, chips in enumerate(batches):
        best = jnp.zeros((slots, list_size), jnp.float32)
        begin = 0
        for stop in (1, 2, 3):
            relayed = relays.get((k, stop), ())
            if relayed or (stop == 3 and 0 < k < 3):
                best = score(k, place, best, begin * step, (stop - begin) * step)
                begin = stop
                for item in relayed:
                    relay(*item)
        ahead = 0 < k < len(batches) - 1
        if ahead:
            complete(k + 1)
            picks, later = choose(batches[k + 1])
        elif k == 0:
            early = choose(batches[1][:direct])
        best = score(k, place, best, begin * step, (4 - begin) * step)
        if ahead:
            after = select(batches[k + 1], picks, picked_refs[(k + 1) % 2])
        encode(k, best, norm)
        if k == 0:
            give_back([back(direct - 1), back(BATCH - 1)])
            complete(1)
            picks, later = join(early, choose(batches[1][direct:]))
            after = select(batches[1], picks, picked_refs[1])
        else:
            give_back(others(k))
        if k == 1:
            give_back([back(n) for n in range(1, BATCH - 1) if n != direct - 1])
        place, norm = later, after
    got_ref[0] = send_ref[0]

    target = jnp.where(lane8 < query_count, (stored >> 5).astype(jnp.float32), -1.0)
    mine = jnp.concatenate([jnp.where(target == d, 1.0, 0.0) for d in order], axis=0)
    rank = ranks(mine)
    spot = jnp.zeros(ids.shape, jnp.float32)
    for n, d in enumerate(order):
        spot = jnp.where(target == d, rank[n * 8 : (n + 1) * 8] + float(n * capacity), spot)
    wide = lax.broadcasted_iota(jnp.int32, (8, devices * capacity), 1).astype(jnp.float32)
    for q in range(0, query_count, 2):
        both = [jnp.where(spot[:, i : i + 1] == wide, 1.0, 0.0) for i in (q, q + 1)]
        place_ref[q * 8 : (q + 2) * 8, :] = jnp.concatenate(both, axis=0).astype(jnp.bfloat16)


    def receive(k):
        for copy in others(k):
            copy.wait_recv()

    def unpack(k, count):
        mine = slice(k * BATCH, (k + count) * BATCH)
        words = got_ref[mine, :capacity, :].reshape(count * slots, LANES)
        codes = [((words >> s) & 255).astype(jnp.float32) for s in (0, 8, 16, 24)]
        codes = jnp.concatenate([p.astype(jnp.bfloat16) for p in codes], axis=1)
        powers = got_ref[mine, capacity : capacity + 1, :].astype(jnp.float32)
        powers = jnp.sum(powers.reshape(count * BATCH // 4, 4, LANES), axis=1)
        powers = jnp.concatenate(
            [jnp.broadcast_to(powers[g : g + 1], (LANES, LANES)) for g in range(powers.shape[0])],
            axis=1,
        ).astype(jnp.bfloat16)
        return codes, powers

    def gather(codes, powers, rows, k):
        place = place_ref[rows, k * slots : k * slots + codes.shape[0]]
        chosen = jnp.dot(place, codes, preferred_element_type=jnp.float32)
        power = lax.dot_general(
            place, powers, (((1,), (1,)), ((), ())), preferred_element_type=jnp.float32
        )
        return jnp.concatenate([chosen, power], axis=1)

    for k in range(len(batches) - 1):
        receive(k)
    final = len(batches) - 1
    total_ref[...] = gather(*unpack(0, final), slice(None), 0)
    receive(final)
    unpacked = unpack(final, 1)
    results = []
    half = out_ref.shape[0] // 2
    for n in range(2):
        rows = slice(n * half, (n + 1) * half)
        total = total_ref[rows, :] + gather(*unpacked, rows, final)
        scale = jnp.exp(total[:, 4 * LANES :] * LN2) * (1.0 / 65535.0)
        for h in range(2):
            low = total[:, 2 * h * LANES : (2 * h + 1) * LANES]
            high = total[:, (2 * h + 1) * LANES : (2 * h + 2) * LANES]
            out_ref[rows, h * LANES : (h + 1) * LANES] = (low + 256.0 * high) * scale
        part_of = pl.ds(n * half, half)
        results.append(pltpu.make_async_copy(out_ref.at[part_of], out_hbm.at[part_of], out_sem.at[n]))
        results[-1].start()
    for copy in sent:
        copy.wait_send()
    for copy in returned:
        copy.wait_send()
    for copy in results:
        copy.wait()


def fused(queries, projection, lists, probes, owner_map):
    query_count, width = queries.shape
    probe_count = probes.shape[1]
    list_count, list_size = lists.shape[0], lists.shape[1]
    devices = PLANES * PLANE
    pairs, slots = query_count * probe_count, devices * CAPACITY
    rows = width // LANES * query_count + TABLE
    hbm = pl.BlockSpec(memory_space=pltpu.HBM)
    owners = owner_map.reshape(-1, LANES)
    words = (devices, CAPACITY + 1, LANES)
    scores = pl.pallas_call(
        fused_kernel,
        out_shape=jax.ShapeDtypeStruct((pairs, list_size), jnp.float32),
        in_specs=[hbm] * 5,
        out_specs=hbm,
        scratch_shapes=[
            pltpu.VMEM(queries.shape, jnp.bfloat16),
            pltpu.VMEM(projection.shape, jnp.bfloat16),
            pltpu.VMEM((probe_count, query_count), jnp.int32),
            pltpu.VMEM(owners.shape, jnp.int32),
            pltpu.VMEM((devices, rows, LANES), jnp.bfloat16),
            pltpu.VMEM(lists.shape, jnp.bfloat16),
            pltpu.VMEM((list_count, list_size), jnp.float32),
            pltpu.VMEM((BATCH * CAPACITY, width), jnp.bfloat16),
            pltpu.VMEM((BATCH * CAPACITY, width), jnp.bfloat16),
            pltpu.VMEM(words, jnp.int32),
            pltpu.VMEM(words, jnp.int32),
            pltpu.VMEM((pairs, slots), jnp.bfloat16),
            pltpu.VMEM((pairs, 5 * LANES), jnp.float32),
            pltpu.VMEM((pairs, list_size), jnp.float32),
            pltpu.SemaphoreType.DMA((4,)),
            pltpu.SemaphoreType.DMA((8,)),
            pltpu.SemaphoreType.DMA((devices,)),
            pltpu.SemaphoreType.DMA((devices,)),
            pltpu.SemaphoreType.DMA((devices,)),
            pltpu.SemaphoreType.DMA((devices,)),
            pltpu.SemaphoreType.DMA((2,)),
        ],
        compiler_params=pltpu.CompilerParams(
            collective_id=0, has_side_effects=True, vmem_limit_bytes=VMEM_LIMIT
        ),
    )(queries, projection, probes.T, owners, lists)
    return scores.reshape(query_count, probe_count, list_size)


def solution(mesh):
    placed = (
        P(AXES, None),
        P(),
        P(AXES, None, None),
        P(AXES, None),
        P(),
    )
    sizes = (mesh.shape["grp"], mesh.shape["own"])
    return jax.shard_map(
        fused if sizes == (8, 4) else general,
        mesh=mesh,
        in_specs=placed,
        out_specs=P(AXES, None, None),
        check_vma=False,
    )
```

```python
import jax
import jax.numpy as jnp
from jax import lax
from jax.experimental import pallas as pl
from jax.experimental.pallas import tpu as pltpu
from jax.sharding import PartitionSpec as P

AXES = ("grp", "own")
LANES = 128
LOG2E = 1.4426950408889634
LN2 = 0.6931471805599453


def select_kernel(queries, width, row_ref, all_ref, out_ref):
    devices = all_ref.shape[0]
    count = out_ref.shape[0]
    numbers = lax.broadcasted_iota(jnp.int32, (count, devices * queries), 1)
    pick = (numbers == row_ref[...]).astype(jnp.float32).astype(jnp.bfloat16)
    for j in range(width // LANES):
        part = all_ref[:, j * queries : (j + 1) * queries, :].reshape(devices * queries, LANES)
        out_ref[:, j * LANES : (j + 1) * LANES] = jnp.dot(
            pick, part, preferred_element_type=jnp.float32
        ).astype(jnp.bfloat16)


def select_rows(everyone, row_of, queries, width):
    slots = row_of.shape[0]
    block = min(256, slots)
    return pl.pallas_call(
        lambda *refs: select_kernel(queries, width, *refs),
        grid=(slots // block,),
        out_shape=jax.ShapeDtypeStruct((slots, width), jnp.bfloat16),
        in_specs=[
            pl.BlockSpec((block, 1), lambda i: (i, 0)),
            pl.BlockSpec(memory_space=pltpu.VMEM),
        ],
        out_specs=pl.BlockSpec((block, width), lambda i: (i, 0)),
        compiler_params=pltpu.CompilerParams(vmem_limit_bytes=48 * 2**20),
    )(row_of[:, None], everyone)


def score_kernel(blocks, rows_ref, lists_ref, spot_ref, out_ref, held):
    step = pl.program_id(0)
    count, list_size, width = lists_ref.shape
    capacity = rows_ref.shape[0] // count
    for n in range(count):
        rows = rows_ref[n * capacity : (n + 1) * capacity, :]
        dots = lax.dot_general(
            rows, lists_ref[n], (((1,), (1,)), ((), ())), preferred_element_type=jnp.float32
        )
        rows_f = rows.astype(jnp.float32)
        row_norm = jnp.sum(rows_f * rows_f, axis=1, keepdims=True)
        partial = None
        for j in range(width // LANES):
            part = lists_ref[n, :, j * LANES : (j + 1) * LANES].astype(jnp.float32)
            partial = part * part if partial is None else partial + part * part
        vec_norm = jnp.sum(partial.T, axis=0, keepdims=True)
        distance = jnp.maximum((row_norm + vec_norm - 2.0 * dots) / width, 0.0)
        largest = jnp.maximum(jnp.max(distance, axis=1, keepdims=True), 1e-30)
        power = jnp.clip(jnp.ceil(jnp.log(largest) * LOG2E + 1e-3), -100.0, 120.0)
        code = jnp.clip(jnp.round(distance * (65535.0 * jnp.exp(power * -LN2))), 0.0, 65535.0)
        high = jnp.floor(code * (1.0 / 256.0))
        low = code - high * 256.0
        place = pl.ds(pl.multiple_of((step * count + n) * capacity, 16), capacity)
        held[place, :list_size] = high.astype(jnp.bfloat16)
        held[place, list_size : 2 * list_size] = low.astype(jnp.bfloat16)
        held[place, 2 * list_size :] = jnp.broadcast_to(power, (capacity, LANES)).astype(
            jnp.bfloat16
        )

    @pl.when(step == pl.num_programs(0) - 1)
    def _():
        slots = held.shape[0]
        each = slots // blocks
        numbers = lax.broadcasted_iota(jnp.int32, (slots, slots), 1)
        pick = (numbers == spot_ref[...]).astype(jnp.float32).astype(jnp.bfloat16)
        got = jnp.dot(pick, held[...], preferred_element_type=jnp.float32)
        code = got[:, :list_size] * 256.0 + got[:, list_size : 2 * list_size] - 32768.0
        parts = [
            code[:, h * LANES : (h + 1) * LANES].reshape(blocks, each, LANES)
            for h in range(list_size // LANES)
        ]
        powers = got[:, 2 * list_size :].reshape(blocks, each, LANES)
        slot = lax.broadcasted_iota(jnp.int32, powers.shape, 1)
        lane = lax.broadcasted_iota(jnp.int32, powers.shape, 2)
        powers = jnp.sum(jnp.where(slot == lane, powers, 0.0), axis=1, keepdims=True)
        parts.append(jnp.broadcast_to(powers, (blocks, 16, LANES)))
        whole = jnp.concatenate(parts, axis=1)
        out_ref[...] = whole.astype(jnp.int32).astype(jnp.int16)


def score(grouped, lists, spot, blocks):
    list_count, list_size, width = lists.shape
    slots = grouped.shape[0]
    count = 4
    out_rows = (slots // blocks) * list_size // LANES + 16
    return pl.pallas_call(
        lambda *refs: score_kernel(blocks, *refs),
        grid=(list_count // count,),
        out_shape=jax.ShapeDtypeStruct((blocks, out_rows, LANES), jnp.int16),
        in_specs=[
            pl.BlockSpec((slots // list_count * count, width), lambda i: (i, 0)),
            pl.BlockSpec((count, list_size, width), lambda i: (i, 0, 0)),
            pl.BlockSpec((slots, 1), lambda i: (0, 0)),
        ],
        out_specs=pl.BlockSpec((blocks, out_rows, LANES), lambda i: (0, 0, 0)),
        scratch_shapes=[pltpu.VMEM((slots, 2 * list_size + LANES), jnp.bfloat16)],
        compiler_params=pltpu.CompilerParams(vmem_limit_bytes=40 * 2**20),
    )(grouped, lists, spot[:, None])


def exchange_kernel(device_count, owner_count, out_ref, in_ref, send_sem, recv_sem):
    me = lax.axis_index("grp") * owner_count + lax.axis_index("own")

    def at(k):
        other = lax.rem(me + k, device_count)
        return other, (other // owner_count, lax.rem(other, owner_count))

    barrier = pltpu.get_barrier_semaphore()

    @pl.loop(1, device_count)
    def _(k):
        pl.semaphore_signal(
            barrier, inc=1, device_id=at(k)[1], device_id_type=pl.DeviceIdType.MESH
        )

    pl.semaphore_wait(barrier, device_count - 1)

    def describe(k, block):
        other, where = at(k)
        return pltpu.make_async_remote_copy(
            src_ref=out_ref.at[other],
            dst_ref=in_ref.at[block],
            send_sem=send_sem.at[k],
            recv_sem=recv_sem.at[block],
            device_id=where,
            device_id_type=pl.DeviceIdType.MESH,
        )

    @pl.loop(1, device_count)
    def _(k):
        describe(k, me).start()

    in_ref[me] = out_ref[me]

    @pl.loop(1, device_count)
    def _(k):
        describe(k, at(k)[0]).wait_recv()

    @pl.loop(1, device_count)
    def _(k):
        describe(k, me).wait_send()


def exchange(blocks):
    owner_count = lax.axis_size("own")
    device_count = blocks.shape[0]
    return pl.pallas_call(
        lambda *refs: exchange_kernel(device_count, owner_count, *refs),
        out_shape=jax.ShapeDtypeStruct(blocks.shape, blocks.dtype),
        in_specs=[pl.BlockSpec(memory_space=pltpu.VMEM)],
        out_specs=pl.BlockSpec(memory_space=pltpu.VMEM),
        scratch_shapes=[
            pltpu.SemaphoreType.DMA((device_count,)),
            pltpu.SemaphoreType.DMA((device_count,)),
        ],
        compiler_params=pltpu.CompilerParams(
            collective_id=1, has_side_effects=True, vmem_limit_bytes=16 * 2**20
        ),
    )(blocks)


def general(queries, projection, lists, probes, owner_map):
    query_count, width = queries.shape
    probe_count = probes.shape[1]
    lists_here, list_size = lists.shape[0], lists.shape[1]
    device_count = lax.axis_size("grp") * lax.axis_size("own")
    pairs = query_count * probe_count
    capacity = 2 * pairs // device_count
    list_capacity = device_count * capacity // lists_here
    slots = device_count * capacity
    me = lax.axis_index(AXES)

    projected = jnp.dot(queries, projection, preferred_element_type=jnp.float32).astype(
        jnp.bfloat16
    )
    stored = jnp.take(owner_map, probes.reshape(-1))
    target = stored // lists_here
    local = stored % lists_here
    to_target = (target[:, None] == jnp.arange(device_count, dtype=jnp.int32)[None, :]).astype(
        jnp.bfloat16
    )
    step = jnp.arange(pairs, dtype=jnp.int32)
    earlier = (step[None, :] < step[:, None]).astype(jnp.bfloat16)
    before = jnp.dot(earlier, to_target, preferred_element_type=jnp.float32)
    rank = jnp.sum(before * to_target.astype(jnp.float32), axis=1).astype(jnp.int32)
    position = target * capacity + rank

    at_rank = (rank[:, None] == jnp.arange(capacity, dtype=jnp.int32)[None, :]).astype(jnp.bfloat16)
    query_of = step // probe_count
    what = jnp.stack([jnp.ones_like(step), query_of, local], axis=0).astype(jnp.bfloat16)
    weighted = to_target.T[None] * what[:, None, :]
    table = jnp.dot(
        weighted.reshape(3 * device_count, pairs), at_rank, preferred_element_type=jnp.float32
    ).reshape(3, device_count, capacity)
    table = jnp.where(table[:1] > 0.5, table[1:], -1.0).astype(jnp.bfloat16)
    columns = width // LANES
    extra = -(-(2 * slots) // (16 * LANES)) * 16
    table = jnp.pad(table.reshape(-1), (0, extra * LANES - 2 * slots)).reshape(extra, LANES)
    stacked = projected.reshape(query_count, columns, LANES).transpose(1, 0, 2)
    stacked = stacked.reshape(columns * query_count, LANES)

    everyone = lax.all_gather(jnp.concatenate([stacked, table], axis=0), AXES, tiled=False)
    tables = everyone[:, columns * query_count :].reshape(device_count, -1)[:, : 2 * slots]
    tables = tables.reshape(device_count, 2, device_count, capacity)
    mine = lax.dynamic_index_in_dim(tables, me, axis=2, keepdims=False).astype(jnp.int32)
    asked_query = mine[:, 0].reshape(-1)
    asked_list = mine[:, 1].reshape(-1)
    row_of = (
        asked_query + query_count * (jnp.arange(slots, dtype=jnp.int32) // capacity)
    )

    in_list = (asked_list[:, None] == jnp.arange(lists_here, dtype=jnp.int32)[None, :]).astype(
        jnp.bfloat16
    )
    place = jnp.arange(slots, dtype=jnp.int32)
    earlier = (place[None, :] < place[:, None]).astype(jnp.bfloat16)
    before = jnp.dot(earlier, in_list, preferred_element_type=jnp.float32)
    order = jnp.sum(before * in_list.astype(jnp.float32), axis=1).astype(jnp.int32)
    valid = asked_list >= 0
    spot = jnp.where(valid, asked_list * list_capacity + order, -1)
    hit = spot[:, None] == jnp.arange(lists_here * list_capacity, dtype=jnp.int32)[None, :]
    grouped_row = jnp.sum(jnp.where(hit, row_of[:, None], 0), axis=0)
    grouped = select_rows(everyone, grouped_row, query_count, width)
    blocks = score(grouped, lists, spot, device_count)
    answer_rows = capacity * list_size // LANES
    got = exchange(blocks).astype(jnp.float32)
    powers = got[:, answer_rows:].reshape(device_count, -1)[:, :capacity].reshape(slots, 1)
    returned = (
        got[:, :answer_rows]
        .reshape(device_count, list_size // LANES, capacity, LANES)
        .transpose(0, 2, 1, 3)
        .reshape(slots, list_size)
    )
    returned = (returned + 32768.0) * (jnp.exp2(powers) / 65535.0)
    return returned[position].reshape(query_count, probe_count, list_size)


PLANES = 4
PLANE = 8
TABLE = 16
BATCH = 8
CAPACITY = 32
VMEM_LIMIT = 56 * 2**20


def number(z, x, y, c):
    return z * PLANE + x * 4 + y * 2 + c


def mesh_id(n):
    return (n // 4, lax.rem(n, 4))


def ranks(mine):
    lane = lax.broadcasted_iota(jnp.int32, mine.shape, 1)
    within = mine
    for reach in (1, 2, 4, 8, 16, 32, 64):
        within = within + jnp.where(lane >= reach, pltpu.roll(within, reach, 1), 0.0)
    totals = jnp.broadcast_to(within[:, LANES - 1 :], mine.shape).reshape(-1, 8, LANES)
    probe = lax.broadcasted_iota(jnp.int32, totals.shape, 1)
    before = totals
    for reach in (1, 2, 4):
        before = before + jnp.where(probe >= reach, pltpu.roll(before, reach, 1), 0.0)
    return within - mine + (before - totals).reshape(mine.shape)


def fused_kernel(
    queries_hbm,
    projection_hbm,
    probes_hbm,
    owner_hbm,
    lists_hbm,
    out_hbm,
    queries_ref,
    projection_ref,
    probes_ref,
    owner_ref,
    all_ref,
    lists_ref,
    norms_ref,
    even_ref,
    odd_ref,
    send_ref,
    got_ref,
    place_ref,
    total_ref,
    out_ref,
    input_sem,
    list_sem,
    spread_send,
    spread_recv,
    back_send,
    back_recv,
    out_sem,
):
    grp, own = lax.axis_index("grp"), lax.axis_index("own")
    z, x, y, c = grp // 2, lax.rem(grp, 2), own // 2, lax.rem(own, 2)
    me = number(z, x, y, c)
    devices = all_ref.shape[0]
    query_count, width = queries_ref.shape
    list_count, list_size = lists_ref.shape[0], lists_ref.shape[1]
    columns = width // LANES
    table_at = columns * query_count
    capacity = CAPACITY

    inputs = [
        pltpu.make_async_copy(src, dst, input_sem.at[i])
        for i, (src, dst) in enumerate(
            (
                (projection_hbm, projection_ref),
                (queries_hbm, queries_ref),
                (probes_hbm, probes_ref),
                (owner_hbm, owner_ref),
            )
        )
    ]
    for copy in inputs:
        copy.start()
    barrier = pltpu.get_barrier_semaphore()

    near, cross, opposite = z + 1 - 2 * lax.rem(z, 2), lax.rem(z + 2, PLANES), PLANES - 1 - z
    xa, ya = x * c + (1 - x) * (1 - c), y * (1 - c) + (1 - y) * c
    xb, yb = x * (1 - c) + (1 - x) * c, y * c + (1 - y) * (1 - c)
    sides = {"o": (x, y), "a": (xa, ya), "b": (xb, yb), "d": (1 - x, 1 - y)}
    sides |= {"x": (1 - x, y), "y": (x, 1 - y)}

    def block_of(p, side, twin=False):
        return number(p, *sides[side], 1 - c if twin else c)

    peer_a, peer_b = block_of(z, "a"), block_of(z, "b")
    peer_near, peer_cross = block_of(near, "o"), block_of(cross, "o")
    sibling = block_of(z, "o", True)
    peers = (peer_cross, peer_a, peer_b, peer_near, sibling)
    for peer in peers:
        pl.semaphore_signal(
            barrier, inc=1, device_id=mesh_id(peer), device_id_type=pl.DeviceIdType.MESH
        )

    part = list_count // list_sem.shape[0]

    def list_copy(n):
        piece = pl.ds(n * part, part)
        return pltpu.make_async_copy(lists_hbm.at[piece], lists_ref.at[piece], list_sem.at[n])

    for copy in inputs:
        copy.wait()
    for n in range(list_sem.shape[0]):
        list_copy(n).start()

    projected = jnp.dot(
        queries_ref[...], projection_ref[...], preferred_element_type=jnp.float32
    ).astype(jnp.bfloat16)
    for j in range(columns):
        all_ref[me, j * query_count : (j + 1) * query_count, :] = projected[
            :, j * LANES : (j + 1) * LANES
        ]
    ids = jnp.concatenate([probes_ref[...], probes_ref[...]], axis=1)
    low, high = ids & (LANES - 1), ids >> 7
    stored = jnp.zeros_like(ids)
    for h in range(owner_ref.shape[0]):
        row = jnp.broadcast_to(owner_ref[h : h + 1, :], ids.shape)
        found = jnp.take_along_axis(row, low, axis=1, mode="promise_in_bounds")
        stored = jnp.where(high == h, found, stored)
    lane8 = lax.broadcasted_iota(jnp.int32, ids.shape, 1)
    table = jnp.where(lane8 < query_count, stored >> 5, stored & 31).astype(jnp.float32)
    all_ref[me, table_at:, :] = jnp.concatenate([table, jnp.zeros_like(table)], axis=0).astype(
        jnp.bfloat16
    )
    pl.semaphore_wait(barrier, len(peers))

    sent = []

    def describe(block, peer, slot):
        return pltpu.make_async_remote_copy(
            src_ref=all_ref.at[block],
            dst_ref=all_ref.at[block],
            send_sem=spread_send.at[slot],
            recv_sem=spread_recv.at[block],
            device_id=mesh_id(peer),
            device_id_type=pl.DeviceIdType.MESH,
        )

    def send(block, *peers):
        for peer in peers:
            copy = describe(block, peer, len(sent))
            copy.start()
            sent.append(copy)

    def arrived(block):
        describe(block, sibling, 0).wait_recv()

    def relay(p, side, *peers):
        arrived(block_of(p, side))
        send(block_of(p, side), *peers)

    send(me, *peers)

    def list_norms(first, last):
        for n in range(first, last):
            list_copy(n).wait()
            rows = []
            for i in range(n * part, (n + 1) * part):
                partial = None
                for j in range(columns):
                    piece = lists_ref[i, :, j * LANES : (j + 1) * LANES].astype(jnp.float32)
                    partial = piece * piece if partial is None else partial + piece * piece
                rows.append(0.5 * jnp.sum(partial.T, axis=0, keepdims=True))
            norms_ref[n * part : (n + 1) * part, :] = jnp.concatenate(rows, axis=0)

    list_norms(0, 5)
    relay(z, "a", sibling, peer_b)
    relay(z, "b", sibling)
    list_norms(5, 7)
    relay(cross, "o", peer_a, peer_b, sibling, peer_near)
    list_norms(7, 8)

    itself = (z, "o")
    batches = (
        (
            itself,
            (z, "x"),
            (z, "y"),
            (cross, "o"),
            (z, "o", True),
            (z, "x", True),
            (z, "y", True),
            (cross, "o", True),
        ),
        (
            (cross, "x"),
            (cross, "y"),
            (opposite, "o"),
            (near, "o"),
            (cross, "x", True),
            (cross, "y", True),
            (opposite, "o", True),
            (near, "o", True),
        ),
        (
            (cross, "d"),
            (cross, "d", True),
            (opposite, "x"),
            (opposite, "x", True),
            (opposite, "y"),
            (opposite, "y", True),
            (near, "x"),
            (near, "x", True),
        ),
        (
            (opposite, "d"),
            (opposite, "d", True),
            (z, "d"),
            (z, "d", True),
            (near, "y"),
            (near, "y", True),
            (near, "d"),
            (near, "d", True),
        ),
    )
    order = [block_of(*where).astype(jnp.float32) for chips in batches for where in chips]
    def back(n):
        return pltpu.make_async_remote_copy(
            src_ref=send_ref.at[n],
            dst_ref=got_ref.at[n],
            send_sem=back_send.at[n],
            recv_sem=back_recv.at[n],
            device_id=mesh_id(block_of(*batches[n // BATCH][n % BATCH])),
            device_id_type=pl.DeviceIdType.MESH,
        )

    me_f = me.astype(jnp.float32)
    slots = BATCH * capacity
    slot = lax.broadcasted_iota(jnp.int32, (capacity, LANES), 0).astype(jnp.float32)

    def choose(chips):
        tables = [
            all_ref[block_of(*where), table_at:, :].astype(jnp.float32)[:8, :] for where in chips
        ]
        tables = jnp.concatenate(tables, axis=0)
        lane = lax.broadcasted_iota(jnp.int32, tables.shape, 1)
        mine = jnp.where((lane < query_count) & (tables == me_f), 1.0, 0.0)
        rank = jnp.where(mine > 0.5, ranks(mine), -1.0)
        local = tables + 1.0
        at = (rank, pltpu.roll(rank, query_count, 1))
        what = (pltpu.roll(local, query_count, 1), local)
        picks, lists_of = [], []
        for t in range(len(chips)):
            pick = jnp.zeros((capacity, LANES), jnp.float32)
            which = jnp.zeros((capacity, LANES), jnp.float32)
            for j in range(8):
                row = t * 8 + j
                hit = at[t % 2][row : row + 1, :] == slot
                pick = jnp.where(hit, 1.0, pick)
                which = jnp.where(hit, what[t % 2][row : row + 1, :], which)
            picks.append(pick.astype(jnp.bfloat16))
            lists_of.append(which)
        place = jnp.sum(jnp.concatenate(lists_of, axis=0), axis=1, keepdims=True)
        place = jnp.broadcast_to(place, (place.shape[0], LANES))
        return picks, place

    def join(one, two):
        return one[0] + two[0], jnp.concatenate([one[1], two[1]], axis=0)

    def select(chips, picks, picked):
        norm = jnp.zeros((slots, LANES), jnp.float32)
        for j in range(columns):
            rows = []
            for u in range(0, BATCH, 2):
                pair = [
                    all_ref[block_of(*where), j * query_count : (j + 1) * query_count, :]
                    for where in chips[u : u + 2]
                ]
                pair = jnp.concatenate(pair, axis=0)
                pick = jnp.concatenate(picks[u : u + 2], axis=0)
                rows.append(jnp.dot(pick, pair, preferred_element_type=jnp.float32))
            piece = jnp.concatenate(rows, axis=0)
            norm = norm + piece * piece
            picked[:, j * LANES : (j + 1) * LANES] = piece.astype(jnp.bfloat16)
        return jnp.sum(norm, axis=1, keepdims=True)

    def encode(k, best, norm):
        distance = jnp.maximum((norm - 2.0 * best) * (1.0 / width), 0.0)
        largest = jnp.maximum(jnp.max(distance, axis=1, keepdims=True), 1e-30)
        power = jnp.clip(jnp.ceil(jnp.log(largest) * LOG2E + 1e-3), -100.0, 120.0)
        code = jnp.clip(jnp.round(distance * (65535.0 * jnp.exp(power * -LN2))), 0.0, 65535.0)
        code = code.astype(jnp.int32)
        word = code[:, :LANES] | (code[:, LANES:] << 16)
        whole = (BATCH, capacity, LANES)
        word = word.reshape(whole)
        quarter = lax.broadcasted_iota(jnp.int32, whole, 0) & 3
        spot = lax.broadcasted_iota(jnp.int32, whole, 1) + quarter * capacity
        lane = lax.broadcasted_iota(jnp.int32, whole, 2)
        powers = jnp.broadcast_to(power, (slots, LANES)).reshape(whole)
        powers = jnp.sum(jnp.where(spot == lane, powers, 0.0), axis=1, keepdims=True)
        powers = powers.astype(jnp.int32)
        send_ref[k * BATCH : (k + 1) * BATCH, :capacity, :] = word
        send_ref[k * BATCH : (k + 1) * BATCH, capacity : capacity + 1, :] = powers

    returned = []

    def others(k):
        return [back(n) for n in range(max(k * BATCH, 1), (k + 1) * BATCH)]

    def give_back(copies):
        for copy in copies:
            copy.start()
            returned.append(copy)

    relays = {
        (0, 2): ((opposite, "o", peer_a, peer_b, sibling),),
        (0, 3): (
            (cross, "a", peer_b, sibling),
            (cross, "b", sibling),
            (z, "d", peer_near, sibling),
        ),
        (1, 2): (
            (opposite, "a", sibling),
            (near, "a", sibling),
            (near, "b", sibling),
            (opposite, "b", sibling),
            (cross, "d", peer_near, sibling),
        ),
        (2, 1): ((near, "d", sibling),),
        (2, 2): ((opposite, "d", sibling),),
    }
    picked_refs = (even_ref, odd_ref)

    def complete(k):
        for where in batches[k]:
            if len(where) == 3:
                arrived(block_of(*where))

    def score(k, place, best, first, count):
        dots = lax.dot_general(
            picked_refs[k % 2][...],
            lists_ref[first : first + count].reshape(count * list_size, width),
            (((1,), (1,)), ((), ())),
            preferred_element_type=jnp.float32,
        )
        for i in range(count):
            n = first + i
            hit = place == n + 1.0
            hit = jnp.concatenate([hit] * (list_size // LANES), axis=1)
            value = dots[:, i * list_size : (i + 1) * list_size] - norms_ref[n : n + 1, :]
            best = jnp.where(hit, value, best)
        return best

    step = list_count // 4
    direct = BATCH // 2
    early = choose(batches[0][:direct])
    complete(0)
    relay(near, "o", sibling, peer_a, peer_b)
    picks, place = join(early, choose(batches[0][direct:]))
    norm = select(batches[0], picks, picked_refs[0])
    for k, chips in enumerate(batches):
        best = jnp.zeros((slots, list_size), jnp.float32)
        begin = 0
        for stop in (1, 2, 3):
            relayed = relays.get((k, stop), ())
            if relayed or (stop == 3 and 0 < k < 3):
                best = score(k, place, best, begin * step, (stop - begin) * step)
                begin = stop
                for item in relayed:
                    relay(*item)
        ahead = 0 < k < len(batches) - 1
        if ahead:
            complete(k + 1)
            picks, later = choose(batches[k + 1])
        elif k == 0:
            early = choose(batches[1][:direct])
        best = score(k, place, best, begin * step, (4 - begin) * step)
        if ahead:
            after = select(batches[k + 1], picks, picked_refs[(k + 1) % 2])
        encode(k, best, norm)
        if k == 0:
            give_back([back(direct - 1), back(BATCH - 1)])
            complete(1)
            picks, later = join(early, choose(batches[1][direct:]))
            after = select(batches[1], picks, picked_refs[1])
        else:
            give_back(others(k))
        if k == 1:
            give_back([back(n) for n in range(1, BATCH - 1) if n != direct - 1])
        place, norm = later, after
    got_ref[0] = send_ref[0]

    target = jnp.where(lane8 < query_count, (stored >> 5).astype(jnp.float32), -1.0)
    mine = jnp.concatenate([jnp.where(target == d, 1.0, 0.0) for d in order], axis=0)
    rank = ranks(mine)
    spot = jnp.zeros(ids.shape, jnp.float32)
    for n, d in enumerate(order):
        spot = jnp.where(target == d, rank[n * 8 : (n + 1) * 8] + float(n * capacity), spot)
    wide = lax.broadcasted_iota(jnp.int32, (8, devices * capacity), 1).astype(jnp.float32)
    for q in range(0, query_count, 2):
        both = [jnp.where(spot[:, i : i + 1] == wide, 1.0, 0.0) for i in (q, q + 1)]
        place_ref[q * 8 : (q + 2) * 8, :] = jnp.concatenate(both, axis=0).astype(jnp.bfloat16)


    def receive(k):
        for copy in others(k):
            copy.wait_recv()

    def unpack(k, count):
        mine = slice(k * BATCH, (k + count) * BATCH)
        words = got_ref[mine, :capacity, :].reshape(count * slots, LANES)
        codes = [((words >> s) & 255).astype(jnp.float32) for s in (0, 8, 16, 24)]
        codes = jnp.concatenate([p.astype(jnp.bfloat16) for p in codes], axis=1)
        powers = got_ref[mine, capacity : capacity + 1, :].astype(jnp.float32)
        powers = jnp.sum(powers.reshape(count * BATCH // 4, 4, LANES), axis=1)
        powers = jnp.concatenate(
            [jnp.broadcast_to(powers[g : g + 1], (LANES, LANES)) for g in range(powers.shape[0])],
            axis=1,
        ).astype(jnp.bfloat16)
        return codes, powers

    def gather(codes, powers, rows, k):
        place = place_ref[rows, k * slots : k * slots + codes.shape[0]]
        chosen = jnp.dot(place, codes, preferred_element_type=jnp.float32)
        power = lax.dot_general(
            place, powers, (((1,), (1,)), ((), ())), preferred_element_type=jnp.float32
        )
        return jnp.concatenate([chosen, power], axis=1)

    for k in range(len(batches) - 1):
        receive(k)
    final = len(batches) - 1
    total_ref[...] = gather(*unpack(0, final), slice(None), 0)
    receive(final)
    unpacked = unpack(final, 1)
    results = []
    half = out_ref.shape[0] // 2
    for n in range(2):
        rows = slice(n * half, (n + 1) * half)
        total = total_ref[rows, :] + gather(*unpacked, rows, final)
        scale = jnp.exp(total[:, 4 * LANES :] * LN2) * (1.0 / 65535.0)
        for h in range(2):
            low = total[:, 2 * h * LANES : (2 * h + 1) * LANES]
            high = total[:, (2 * h + 1) * LANES : (2 * h + 2) * LANES]
            out_ref[rows, h * LANES : (h + 1) * LANES] = (low + 256.0 * high) * scale
        part_of = pl.ds(n * half, half)
        results.append(pltpu.make_async_copy(out_ref.at[part_of], out_hbm.at[part_of], out_sem.at[n]))
        results[-1].start()
    for copy in sent:
        copy.wait_send()
    for copy in returned:
        copy.wait_send()
    for copy in results:
        copy.wait()


def fused(queries, projection, lists, probes, owner_map):
    query_count, width = queries.shape
    probe_count = probes.shape[1]
    list_count, list_size = lists.shape[0], lists.shape[1]
    devices = PLANES * PLANE
    pairs, slots = query_count * probe_count, devices * CAPACITY
    rows = width // LANES * query_count + TABLE
    hbm = pl.BlockSpec(memory_space=pltpu.HBM)
    owners = owner_map.reshape(-1, LANES)
    words = (devices, CAPACITY + 1, LANES)
    scores = pl.pallas_call(
        fused_kernel,
        out_shape=jax.ShapeDtypeStruct((pairs, list_size), jnp.float32),
        in_specs=[hbm] * 5,
        out_specs=hbm,
        scratch_shapes=[
            pltpu.VMEM(queries.shape, jnp.bfloat16),
            pltpu.VMEM(projection.shape, jnp.bfloat16),
            pltpu.VMEM((probe_count, query_count), jnp.int32),
            pltpu.VMEM(owners.shape, jnp.int32),
            pltpu.VMEM((devices, rows, LANES), jnp.bfloat16),
            pltpu.VMEM(lists.shape, jnp.bfloat16),
            pltpu.VMEM((list_count, list_size), jnp.float32),
            pltpu.VMEM((BATCH * CAPACITY, width), jnp.bfloat16),
            pltpu.VMEM((BATCH * CAPACITY, width), jnp.bfloat16),
            pltpu.VMEM(words, jnp.int32),
            pltpu.VMEM(words, jnp.int32),
            pltpu.VMEM((pairs, slots), jnp.bfloat16),
            pltpu.VMEM((pairs, 5 * LANES), jnp.float32),
            pltpu.VMEM((pairs, list_size), jnp.float32),
            pltpu.SemaphoreType.DMA((4,)),
            pltpu.SemaphoreType.DMA((8,)),
            pltpu.SemaphoreType.DMA((devices,)),
            pltpu.SemaphoreType.DMA((devices,)),
            pltpu.SemaphoreType.DMA((devices,)),
            pltpu.SemaphoreType.DMA((devices,)),
            pltpu.SemaphoreType.DMA((2,)),
        ],
        compiler_params=pltpu.CompilerParams(
            collective_id=0, has_side_effects=True, vmem_limit_bytes=VMEM_LIMIT
        ),
    )(queries, projection, probes.T, owners, lists)
    return scores.reshape(query_count, probe_count, list_size)


def solution(mesh):
    placed = (
        P(AXES, None),
        P(),
        P(AXES, None, None),
        P(AXES, None),
        P(),
    )
    sizes = (mesh.shape["grp"], mesh.shape["own"])
    return jax.shard_map(
        fused if sizes == (8, 4) else general,
        mesh=mesh,
        in_specs=placed,
        out_specs=P(AXES, None, None),
        check_vma=False,
    )
```
